32 devices in a mesh: group: 4 (over y, x), expert: 8 (over z, core).
Axes of the slice: x: 2, y: 2, z: 4, core: 2. Of those that a mesh axis runs over, the one named last changes fastest.
Arguments:
- tokens: bfloat16 [32768, 768], P(('group', 'expert')), may hold values from -6 to 6
- cotangent: bfloat16 [32768, 768], P(('group', 'expert')), may hold values from -6 to 6
- norm_attn: bfloat16 [768], P('expert'), may hold values from 0.5 to 1.5
- w_query: bfloat16 [768, 768], P('expert'), may hold values from -0.21875 to 0.21875
- w_key: bfloat16 [768, 768], P('expert'), may hold values from -0.21875 to 0.21875
- w_value: bfloat16 [768, 768], P('expert'), may hold values from -0.21875 to 0.21875
- w_out: bfloat16 [768, 768], P('expert'), may hold values from -0.875 to 0.875
- rel_bias: bfloat16 [384], P('expert'), may hold values from -4 to 4
- norm_expert: bfloat16 [768], P('expert'), may hold values from 0.5 to 1.5
- w_router: bfloat16 [768, 8], P('expert'), may hold values from -0.14941406 to 0.14941406
- expert_in: bfloat16 [8, 768, 3072], P('expert'), may hold values from -0.21875 to 0.21875
- expert_out: bfloat16 [8, 3072, 768], P('expert'), may hold values from -0.109375 to 0.109375
- expert_ids: int32 [32768, 2], P(('group', 'expert')), may hold values from 0 to 7, all different within a row; in each aligned block of 512 rows (0 to 511, 512 to 1023, ...) at most 192 rows name the same one
- span_starts: int32 [64], P(('group', 'expert')), may hold values from 0 to 256
Outputs:
- mixed: bfloat16 [32768, 768], P(('group', 'expert'))
- grad_tokens: bfloat16 [32768, 768], P(('group', 'expert'))
- grad_norm_attn: float32 [768], P('expert')
- grad_w_query: float32 [768, 768], P('expert')
- grad_w_key: float32 [768, 768], P('expert')
- grad_w_value: float32 [768, 768], P('expert')
- grad_w_out: float32 [768, 768], P('expert')
- grad_rel_bias: float32 [384], P('expert')
- grad_norm_expert: float32 [768], P('expert')
- grad_w_router: float32 [768, 8], P('expert')
- grad_expert_in: float32 [8, 768, 3072], P('expert')
- grad_expert_out: float32 [8, 3072, 768], P('expert')
The draws below stay inside these ranges and needn't reach their ends.
Inputs may be any that keep to these rules, and one draw needn't show every extreme that they name: `expert_ids`: in each aligned block of 512 rows no expert is named by more than 192 rows, a bound that some block reaches; the 2 experts of a row differ.
All inputs are finite; a program needn't handle non-finite values.
Results may differ from the reference program's by a relative error of at most 0.015.
Values may be sent and summed in bfloat16 or wider, within the bound.
No kernel may reach another device: no remote copies, remote signals or barrier semaphores. Data moves between devices by JAX's collectives and lax.ppermute only.
A program may use at most 256 MiB of HBM per device.

```python
import math
import jax
import jax.numpy as jnp
import numpy as np
from jax import lax

D = 768
HEADS = 12
HEAD_DIM = 64
FF = 3072
TOP = 2
BUCKETS = 32
SEQ_LEN = 512
PIC = 256
TOK_MB = 512
TOKENS = 32768
SEQS = 64
EXPERTS = 8
CAP = 192
BIASES = 384


def touch_ends(entries, own_key, smallest, high):
    longest = entries.shape.index(max(entries.shape))
    spots = []
    for shift in (0, 1):
        where = [jax.random.randint(jax.random.fold_in(own_key, axis), (), 0, length) for axis, length in enumerate(entries.shape)]
        where[longest] = (where[longest] + shift) % entries.shape[longest]
        spots.append(tuple(where))
    return entries.at[spots[0]].set(smallest).at[spots[1]].set(high)


def shard_levels(rng, dims, cuts, smallest, top_value):
    factor_of, own = 1.0, jax.random.fold_in(rng, 6)
    for dim, blocks in cuts:
        steps = jnp.exp(jax.random.uniform(jax.random.fold_in(own, dim), (blocks,), jnp.float32, smallest / len(cuts), top_value / len(cuts)))
        factor_of = factor_of * jnp.repeat(steps, dims[dim] // blocks).reshape([-1 if axis == dim else 1 for axis in range(len(dims))])
    return factor_of


def deal_out(rng, own, number, rows, number_of, top, most, skew):
    sequence = jax.random.permutation(rng, number_of)
    heavy_load, usual = shares(number_of, rows * top, most, skew, True), shares(number_of, rows * top, most, skew, False)
    places = jnp.arange(number_of)

    def named(sizes, turn):
        used = int((sizes > 0).sum())
        fixed = max(1, used // 4)
        passed = fixed + (places - fixed + turn * (used - fixed)) % max(1, number_of - fixed)
        return jnp.zeros((number_of,), jnp.int32).at[sequence[jnp.where(places < fixed, places, passed)]].set(jnp.asarray(sizes, jnp.int32))

    sizes = jnp.where(number % 4 == 0, named(heavy_load, number // 4), named(usual, number - number // 4 - 1))
    mixed = jax.random.permutation(jax.random.fold_in(own, 3), number_of)
    donor, taker = mixed[0:number_of // 2 * 2:2], mixed[1:number_of // 2 * 2:2]
    margin = jnp.minimum(sizes[donor] - 1, most - sizes[taker]) // 2
    margin = jnp.where((donor == sequence[0]) | (taker == sequence[0]) | (sizes[taker] == 0), 0, jnp.maximum(margin, 0))
    passed = jax.random.randint(jax.random.fold_in(own, 4), (number_of // 2,), 0, 1 << 20) % (margin + 1)
    sizes = sizes.at[donor].add(-passed).at[taker].add(passed)
    members = jnp.searchsorted(jnp.cumsum(sizes), jnp.arange(rows * top), side="right").astype(jnp.int32)
    grid = members.reshape(top, rows).T
    grid = grid[jax.random.permutation(jax.random.fold_in(own, 1), rows)]
    turn = jax.random.randint(jax.random.fold_in(own, 2), (rows, 1), 0, top)
    return jnp.take_along_axis(grid, (jnp.arange(top)[None, :] + turn) % top, axis=1)


def shares(number_of, total, bound, skew, full):
    loads = [(1 << 20) // math.isqrt(standing ** skew) + 1 for standing in range(1, number_of + 1)]
    largest = bound if full else min(bound, max(-(-total // number_of), total * loads[0] // sum(loads)))
    least = 1 if total - largest >= number_of - 1 else 0
    counts, spare = [largest] + [least] * (number_of - 1), total - largest - least * (number_of - 1)
    while spare > 0:
        movable = [i for i in range(1, number_of) if counts[i] < largest] or [i for i in range(1, number_of) if counts[i] < bound]
        whole, budget = sum([loads[i] for i in movable]), spare
        for i in movable:
            addition = min(bound - counts[i], max(1, budget * loads[i] // whole), spare)
            counts[i] = counts[i] + addition
            spare = spare - addition
    return np.array(counts)


def scatter_about(own_key, extent, width, reach, cuts=(), kind=jnp.bfloat16):
    level = shard_levels(own_key, extent, cuts, -0.22, 0.18) if cuts else 1.0
    result = jax.random.normal(own_key, extent, jnp.float32) * width * level
    return jnp.minimum(jnp.maximum(result, -reach), reach).astype(kind)


def setup_inputs(seed: int = 0) -> dict:
    arg_keys = jax.random.split(jax.random.key(seed), 15)
    tokens = scatter_about(arg_keys[0], (TOKENS, D), 1.0, 6.0, ((0, 32),))
    cotangent = scatter_about(arg_keys[1], (TOKENS, D), 1.0, 6.0, ((0, 32),))
    norm_attn = jnp.clip(1.0 + 0.1 * jax.random.normal(arg_keys[2], (D,), jnp.float32), 0.5, 1.5).astype(jnp.bfloat16)
    w_query = scatter_about(arg_keys[3], (D, D), D ** -0.5, 0.21875, ((0, 8),))
    w_key = scatter_about(arg_keys[4], (D, D), D ** -0.5, 0.21875, ((0, 8),))
    w_value = scatter_about(arg_keys[5], (D, D), D ** -0.5, 0.21875, ((0, 8),))
    w_out = scatter_about(arg_keys[6], (D, D), (D // 16) ** -0.5, 0.875, ((0, 8),))
    rel_bias = scatter_about(arg_keys[7], (BIASES,), 1.0, 4.0, ((0, 8),))
    norm_expert = jnp.clip(1.0 + 0.1 * jax.random.normal(arg_keys[8], (D,), jnp.float32), 0.5, 1.5).astype(jnp.bfloat16)
    w_router = scatter_about(arg_keys[9], (D, EXPERTS), 0.025, 0.14941406, ((0, 8),))
    expert_in = scatter_about(arg_keys[10], (EXPERTS, D, FF), D ** -0.5, 0.21875, ((0, 8),))
    expert_out = scatter_about(arg_keys[11], (EXPERTS, FF, D), FF ** -0.5, 0.109375, ((0, 8),))
    expert_ids_keys = jax.random.split(jax.random.fold_in(arg_keys[12], 1), TOKENS // TOK_MB)
    expert_ids_turns = jax.random.permutation(jax.random.fold_in(arg_keys[12], 3), TOKENS // TOK_MB)
    expert_ids = jax.vmap(lambda own, number: deal_out(jax.random.fold_in(arg_keys[12], 2), own, number, TOK_MB, EXPERTS, TOP, CAP, 2))(expert_ids_keys, expert_ids_turns).reshape((TOKENS, TOP))
    span_starts = touch_ends(jax.random.randint(arg_keys[13], (SEQS,), 0, SEQ_LEN - PIC + 1), jax.random.fold_in(arg_keys[13], 1), 0, SEQ_LEN - PIC).astype(jnp.int32)
    return {"tokens": tokens, "cotangent": cotangent, "norm_attn": norm_attn, "w_query": w_query, "w_key": w_key, "w_value": w_value, "w_out": w_out, "rel_bias": rel_bias, "norm_expert": norm_expert, "w_router": w_router, "expert_in": expert_in, "expert_out": expert_out, "expert_ids": expert_ids, "span_starts": span_starts}


epsilon = 1e-06
bucket_edges = (1, 2, 3, 4, 5, 6, 7, 8, 12, 16, 23, 32, 45, 64, 91)
highest = lax.Precision.HIGHEST

@jax.custom_vjp
def low(v):
    return lax.optimization_barrier(v.astype(jnp.bfloat16)).astype(jnp.float32)

@jax.custom_vjp
def low_back(v):
    return v

def low_keep(v):
    return (low(v), None)

def low_pass(kept, grad):
    return (grad,)

def back_keep(v):
    return (v, None)

def back_low(kept, grad):
    return (low(grad),)
low.defvjp(low_keep, low_pass)
low_back.defvjp(back_keep, back_low)

def bucket_index(offset):
    magnitude = jnp.zeros(offset.shape, jnp.int32)
    for edge in bucket_edges:
        magnitude = magnitude + (jnp.abs(offset) >= edge).astype(jnp.int32)
    return magnitude + 16 * (offset > 0).astype(jnp.int32)

def rms_norm(values, gain):
    return values * lax.rsqrt(lax.optimization_barrier(jnp.mean(values * values, axis=-1, keepdims=True)) + epsilon) * gain

def allowed_mask(start):
    places = jnp.arange(SEQ_LEN, dtype=jnp.int32)
    causal = places[None, :] <= places[:, None]
    inside = (places >= start) & (places < start + PIC)
    return causal | inside[:, None] & inside[None, :]

def gelu_tanh(inner):
    return jax.nn.gelu(inner, approximate=True)

def attend_group(normed, starts, w_query, w_key, w_value, table_bias):
    count = normed.shape[0]

    def project(weight):
        product = jnp.einsum('gld,de->gle', normed, weight, precision=highest)
        return low(low_back(product)).reshape(count, SEQ_LEN, HEADS, HEAD_DIM)
    query = project(w_query)
    keys = project(w_key)
    values = project(w_value)
    scores = jnp.einsum('gqhd,gkhd->ghqk', query, keys, precision=highest) * HEAD_DIM ** (-0.5)
    logits = low_back(scores + table_bias[None])
    allowed = jax.vmap(allowed_mask)(starts)
    masked = jnp.where(allowed[:, None], logits, -1e+30)
    probs = low(jax.nn.softmax(masked, axis=-1))
    mixed = jnp.einsum('ghqk,gkhd->gqhd', probs, values, precision=highest)
    return low(low_back(mixed.reshape(count, SEQ_LEN, D)))

def route_tables(expert_ids):
    blocks_count = TOKENS // TOK_MB
    pairs = expert_ids.reshape(blocks_count, TOK_MB * TOP)
    onehot = (pairs[:, :, None] == jnp.arange(EXPERTS, dtype=jnp.int32)[None, None, :]).astype(jnp.int32)
    before = jnp.cumsum(onehot, axis=1) - onehot
    position = lax.optimization_barrier(jnp.sum(before * onehot, axis=-1))
    block_ids = jnp.arange(blocks_count, dtype=jnp.int32)[:, None]
    slot_global = pairs * (blocks_count * CAP) + block_ids * CAP + position
    owners = jnp.arange(TOKENS * TOP, dtype=jnp.int32) // TOP
    table = jnp.full((EXPERTS * blocks_count * CAP,), TOKENS, jnp.int32)
    table = table.at[slot_global.reshape(-1)].set(owners)
    return (slot_global.reshape(TOKENS, TOP), table.reshape(EXPERTS, blocks_count * CAP))

def reference(tokens, cotangent, norm_attn, w_query, w_key, w_value, w_out, rel_bias, norm_expert, w_router, expert_in, expert_out, expert_ids, span_starts):
    slot_global, index_table = route_tables(expert_ids)
    group = math.gcd(SEQS, max(1, 4096 // SEQ_LEN))
    places = jnp.arange(SEQ_LEN, dtype=jnp.int32)
    buckets = bucket_index(places[None, :] - places[:, None])
    starts = span_starts.reshape(SEQS // group, group)

    def forward(inputs, gain_attn, query_w, key_w, value_w, out_w, bias_w, gain_expert, router_w, inner_w, outer_w):
        normed = low(rms_norm(inputs, gain_attn))
        table_bias = bias_w.reshape(HEADS, BUCKETS)[:, buckets]
        blocks = normed.reshape(SEQS // group, group, SEQ_LEN, D)

        def one_group(element):
            return attend_group(element[0], element[1], query_w, key_w, value_w, table_bias)
        attended = lax.map(jax.checkpoint(one_group), (blocks, starts)).reshape(TOKENS, D)
        hidden = inputs + low_back(jnp.dot(attended, out_w, precision=highest))
        expert_rows = low(rms_norm(hidden, gain_expert))
        router = low_back(jnp.dot(expert_rows, router_w, precision=highest))
        gates = jax.nn.softmax(jnp.take_along_axis(router, expert_ids, axis=1), axis=-1)
        padded = jnp.concatenate([expert_rows, jnp.zeros((1, D), jnp.float32)], axis=0)

        def one_expert(element):
            rows = low_back(padded[element[0]])
            inner = low_back(jnp.dot(rows, element[1], precision=highest))
            active = low(gelu_tanh(inner))
            return low(low_back(jnp.dot(active, element[2], precision=highest)))
        results = lax.map(jax.checkpoint(one_expert), (index_table, inner_w, outer_w))
        picked = results.reshape(-1, D)[slot_global]
        return hidden + lax.optimization_barrier(jnp.sum(gates[:, :, None] * picked, axis=1))
    floats = [array_in.astype(jnp.float32) for array_in in (tokens, norm_attn, w_query, w_key, w_value, w_out, rel_bias, norm_expert, w_router, expert_in, expert_out)]
    mixed, pull = jax.vjp(forward, *floats)
    grads = pull(cotangent.astype(jnp.float32))
    return (mixed.astype(jnp.bfloat16), grads[0].astype(jnp.bfloat16), grads[1], grads[2], grads[3], grads[4], grads[5], grads[6], grads[7], grads[8], grads[9], grads[10])
```

```python
import functools

import jax
import jax.numpy as jnp
import numpy as np
from jax import lax
from jax.experimental import pallas as pl
from jax.experimental.pallas import tpu as pltpu
from jax.sharding import PartitionSpec as P

D = 768
HEADS = 12
HEAD_DIM = 64
FF = 3072
TOP = 2
BUCKETS = 32
SEQ_LEN = 512
PIC = 256
MICRO = 2
TOK_MB = 512
ROW_TILE = 256
DIRECT_MAX = 8
COST_BYTES = 3600000

epsilon = 1e-06
bucket_edges = (1, 2, 3, 4, 5, 6, 7, 8, 12, 16, 23, 32, 45, 64, 91)
f32 = jnp.float32
bf16 = jnp.bfloat16
MIB = 1 << 20


def dot_nn(left, right):
    return lax.dot_general(left, right, (((1,), (0,)), ((), ())), preferred_element_type=f32)


def dot_nt(left, right):
    return lax.dot_general(left, right, (((1,), (1,)), ((), ())), preferred_element_type=f32)


def dot_tn(left, right):
    return lax.dot_general(left, right, (((0,), (0,)), ((), ())), preferred_element_type=f32)


def iota(shape, dim):
    return lax.broadcasted_iota(jnp.int32, shape, dim)


def diagonal_offsets():
    place = np.arange(1024)
    return np.where(place < 896, 384 - place, 1408 - place)


def bucket_hot():
    offset = diagonal_offsets()
    magnitude = sum((np.abs(offset) >= edge).astype(np.int32) for edge in bucket_edges)
    bucket = magnitude + 16 * (offset > 0)
    hot = bucket[None, :] == np.arange(BUCKETS)[:, None]
    return hot & (np.abs(offset) < SEQ_LEN)[None, :]


def lasting(microseconds):
    return pl.CostEstimate(flops=0, bytes_accessed=int(microseconds * COST_BYTES), transcendentals=0)


def resident(shape, index):
    return pl.BlockSpec(shape, index, pipeline_mode=pl.Buffered(1))


def split_rows(values):
    high = values.astype(bf16).astype(f32)
    row = iota((8, values.shape[1]), 0)
    return jnp.where(row == 0, high, jnp.where(row == 1, values - high, 0.0)).astype(bf16)


def row_to_column(row):
    size = row.shape[1]
    step = 128 if size % 128 == 0 else size
    eye = iota((step, step), 0) == iota((step, step), 1)
    columns = [
        jnp.sum(jnp.where(eye, row[:, i : i + step], 0.0), axis=1, keepdims=True)
        for i in range(0, size, step)
    ]
    return columns[0] if len(columns) == 1 else jnp.concatenate(columns, axis=0)


def column_to_row(column):
    size = column.shape[0]
    step = 128 if size % 128 == 0 else size
    eye = iota((step, step), 0) == iota((step, step), 1)
    rows = [
        jnp.sum(jnp.where(eye, column[i : i + step], 0.0), axis=0, keepdims=True)
        for i in range(0, size, step)
    ]
    return rows[0] if len(rows) == 1 else jnp.concatenate(rows, axis=1)


def slot_hot(slot_row, first, size):
    return iota((size, TOK_MB), 0) + first == slot_row


def route_kernel(me_ref, ids_ref, cot_ref, slots_ref, *block_refs, experts, capacity):
    place = iota((experts, TOK_MB), 0)
    earlier = earlier_places()
    for step in range(MICRO):
        here = slice(step * TOK_MB, (step + 1) * TOK_MB)
        hots = [ids_ref[k : k + 1, here] == place for k in range(TOP)]
        both = jnp.where(hots[0] | hots[1], 1.0, 0.0).astype(bf16)
        at = dot_nn(both, earlier) + ((place ^ me_ref[0]) * capacity).astype(f32)
        slots = [jnp.sum(jnp.where(hot, at, 0.0), axis=0, keepdims=True).astype(jnp.int32) for hot in hots]
        for k in range(TOP):
            slots_ref[step, k : k + 1, :] = slots[k]
        rows = block_refs[0].shape[0] // MICRO
        half = min(rows // 2, 384)
        for first in range(0, experts * capacity, half):
            hot = slot_hot(slots[0], first, half) | slot_hot(slots[1], first, half)
            value = dot_nn(jnp.where(hot, 1.0, 0.0).astype(bf16), cot_ref[here, :]).astype(bf16)
            index, low = first // rows, first % rows
            if len(block_refs) > 1:
                low = 2 * low + step * half
            else:
                low = low + step * rows
            block_refs[index][low : low + half, :] = value


def earlier_places():
    return jnp.where(iota((TOK_MB, TOK_MB), 0) < iota((TOK_MB, TOK_MB), 1), 1.0, 0.0).astype(bf16)


def route(me, ids, cotangent, blocks, experts, capacity):
    size = MICRO * experts * capacity // blocks
    return pl.pallas_call(
        functools.partial(route_kernel, experts=experts, capacity=capacity),
        in_specs=[pl.BlockSpec(memory_space=pltpu.SMEM)] + [pl.BlockSpec(memory_space=pltpu.VMEM)] * 2,
        out_shape=[jax.ShapeDtypeStruct((MICRO, TOP, TOK_MB), jnp.int32)]
        + [jax.ShapeDtypeStruct((size, D), bf16)] * blocks,
        compiler_params=pltpu.CompilerParams(vmem_limit_bytes=32 * MIB),
        cost_estimate=lasting(4),
        name="route",
    )(me, ids, cotangent)


def partner_kernel(me_ref, ids_ref, other_ref, *, xor):
    devices, capacity = other_ref.shape[1:]
    earlier = earlier_places()
    mine = me_ref[0].astype(f32)
    for step in range(MICRO):
        first, second = ids_ref[step], ids_ref[MICRO + step]
        hot = (first == mine) | (second == mine)
        order = dot_nn(jnp.where(hot, 1.0, 0.0).astype(bf16), earlier).astype(jnp.int32)
        order = jnp.where(hot, order, -1)
        partner = (first + second - mine).astype(bf16)
        for sender in range(devices):
            pick = jnp.where(iota((capacity, TOK_MB), 0) == order[sender : sender + 1, :], 1.0, 0.0).astype(bf16)
            found = dot_nt(partner, pick)[sender : sender + 1, :]
            row = sender ^ me_ref[0] if xor else sender
            other_ref[step, pl.ds(row, 1), :] = found


def partners(me, ids, devices, capacity, xor):
    return pl.pallas_call(
        functools.partial(partner_kernel, xor=xor),
        in_specs=[pl.BlockSpec(memory_space=pltpu.SMEM)] + [pl.BlockSpec(memory_space=pltpu.VMEM)],
        out_shape=jax.ShapeDtypeStruct((MICRO, devices, capacity), f32),
        compiler_params=pltpu.CompilerParams(vmem_limit_bytes=32 * MIB),
        cost_estimate=lasting(1.3),
        name="partners",
    )(me, ids)


def unpack_kernel(place_ref, *refs, groups, chips, lines):
    own, passed, small, (out_ref, narrow_ref, ids_ref) = refs[:groups], refs[groups], refs[groups + 1], refs[groups + 2 :]
    rows = own[0].shape[0] // chips
    me = place_ref[1]
    for k in range(groups):
        for j in range(chips):
            low = (k * chips + j) * rows
            values = own[k][j * rows : (j + 1) * rows, :], passed[low : low + rows, :]
            for core in range(2):
                here = pl.ds(pl.multiple_of((me ^ (2 * j + core)) * rows, rows), rows)
                out_ref[place_ref[0] ^ k, here, :] = values[core]
    gathered = jnp.zeros((16, D), f32)
    lane = iota((16, D), 1)
    for k in range(2 * chips):
        source = small if k % 2 == 0 else passed
        low = k // 2 * 16 + (0 if k % 2 == 0 else groups * chips * rows)
        block = source[low : low + 16, :].astype(f32)
        device = me ^ k
        gathered = gathered + pltpu.roll(jnp.where(lane < rows, block, 0.0), device * rows, 1)
        for pick in range(TOP * MICRO):
            ids_ref[pick, pl.ds(device, 1), :] = block[lines + pick : lines + pick + 1, :TOK_MB]
    narrow_ref[...] = gathered.astype(bf16)


def gather_weights(matrices, narrow, ids, groups, devices):
    lines, shard = narrow.shape
    if devices > DIRECT_MAX:
        whole = jnp.stack([lax.all_gather(w, "expert", axis=0, tiled=True) for w in matrices])
        flat = jnp.concatenate([narrow.reshape(-1), ids.astype(bf16).reshape(-1)])
        flat = lax.all_gather(flat, "expert", axis=0)
        narrow = flat[:, : lines * shard].reshape(devices, lines, shard).transpose(1, 0, 2).reshape(lines, D)
        ids = flat[:, lines * shard :].astype(f32).reshape(devices, TOP * MICRO, TOK_MB).transpose(1, 0, 2)
        return whole, narrow, ids
    chips = devices // 2
    group, me = lax.axis_index("group"), lax.axis_index("expert")
    mine = matrices[0]
    for index in range(1, groups):
        mine = jnp.where(group == index, matrices[index], mine)
    small = jnp.concatenate(
        [
            jnp.pad(narrow, ((0, 0), (0, D - shard))),
            jnp.pad(ids.astype(bf16).reshape(TOP * MICRO, TOK_MB), ((0, 0), (0, D - TOK_MB))),
            jnp.zeros((16 - lines - TOP * MICRO, D), bf16),
        ],
        axis=0,
    )
    mine = jnp.concatenate([mine, small], axis=0)
    mine = [mine] + [lax.ppermute(mine, "expert", swap(devices, 2 * j)) for j in range(1, chips)]
    small = jnp.concatenate([m[shard:] for m in mine], axis=0)
    mine = jnp.concatenate([m[:shard] for m in mine], axis=0)
    own = [mine] + [lax.ppermute(mine, "group", swap(groups, k)) for k in range(1, groups)]
    passed = lax.ppermute(jnp.concatenate([*own, small], axis=0), "expert", swap(devices, 1))
    place = jnp.stack([group, me]).astype(jnp.int32)
    return pl.pallas_call(
        functools.partial(unpack_kernel, groups=groups, chips=chips, lines=lines),
        in_specs=[pl.BlockSpec(memory_space=pltpu.SMEM)] + [pl.BlockSpec(memory_space=pltpu.VMEM)] * (groups + 2),
        out_shape=[
            jax.ShapeDtypeStruct((groups, D, D), bf16),
            jax.ShapeDtypeStruct((16, D), bf16),
            jax.ShapeDtypeStruct((TOP * MICRO, devices, TOK_MB), f32),
        ],
        compiler_params=pltpu.CompilerParams(vmem_limit_bytes=32 * MIB),
        cost_estimate=lasting(3),
        name="unpack",
    )(place, *own, passed, small)


def swap(devices, mask):
    return [(i, i ^ mask) for i in range(devices)]


def bias_places(devices):
    place = np.arange(D)
    wide, share = D // devices, HEADS * BUCKETS // devices
    flat = place // wide * share + place % wide
    used = place % wide < share
    bucket = (flat[:, None] % BUCKETS == np.arange(BUCKETS)[None, :]) & used[:, None]
    head = (flat[None, :] // BUCKETS == np.arange(16)[:, None]) & used[None, :]
    return bucket.astype(np.float32), head.astype(np.float32)


def attend_kernel(
    starts_ref, x_ref, query_w, key_w, value_w, out_w, narrow_ref, hot_ref, bucket_ref, heads_ref, ids_ref, slots_ref,
    query_ref, key_ref, value_ref, probs_ref, attended_ref, hidden_ref, rows_ref, gates_ref, normed_ref,
    *refs, step, experts,
):
    block_refs, (mask_ref, table_ref) = refs[:-2], refs[-2:]
    head = pl.program_id(0)

    @pl.when(head == 0)
    def _():
        x = x_ref[...].astype(f32)
        scale = lax.rsqrt(jnp.mean(x * x, axis=-1, keepdims=True) + epsilon)
        normed = (x * scale * narrow_ref[experts : experts + 1, :].astype(f32)).astype(bf16)
        normed_ref[...] = normed
        query = dot_nn(normed, query_w[0]).astype(bf16).astype(f32) * HEAD_DIM**-0.5
        query_ref[...] = query.T.astype(bf16)
        key_ref[...] = dot_nn(normed, key_w[0]).T.astype(bf16)
        value_ref[...] = dot_nn(normed, value_w[0]).T.astype(bf16)
        rel = (heads_ref[...].astype(f32) * narrow_ref[experts + 2 : experts + 3, :].astype(f32)).astype(bf16)
        table_ref[...] = dot_nn(dot_nn(rel, bucket_ref[...]).astype(bf16), hot_ref[...])
        start = starts_ref[step]
        key_place, query_place = iota((SEQ_LEN, SEQ_LEN), 0), iota((SEQ_LEN, SEQ_LEN), 1)
        inside = (
            (key_place >= start)
            & (key_place < start + PIC)
            & (query_place >= start)
            & (query_place < start + PIC)
        )
        mask_ref[...] = jnp.where((key_place <= query_place) | inside, 0.0, -1e30)

    span = pl.ds(pl.multiple_of(head * HEAD_DIM, HEAD_DIM), HEAD_DIM)
    table = jnp.broadcast_to(table_ref[pl.ds(head, 1), :], (8, 1024))
    low_row = iota((8, 1024), 0)
    for bit in (1, 2, 4):
        table = jnp.where((low_row & bit) != 0, pltpu.roll(table, bit, 1), table)
    for shift in (8, 16, 32, 64):
        table = jnp.concatenate([table, pltpu.roll(table, shift, 1)], axis=0)
    scores = dot_tn(key_ref[span, :], query_ref[span, :])
    bias = jnp.concatenate([table[:, 384 - a * 128 : 896 - a * 128] for a in range(4)], axis=0)
    scores = scores + bias + mask_ref[...]
    expo = jnp.exp(scores - jnp.max(scores, axis=0, keepdims=True))
    probs = (expo * (1.0 / jnp.sum(expo, axis=0, keepdims=True))).astype(bf16)
    probs_ref[0] = probs
    attended_ref[span, :] = dot_nn(value_ref[span, :], probs).astype(bf16)

    @pl.when(head == HEADS - 1)
    def _():
        hidden = x_ref[...].astype(f32) + dot_tn(attended_ref[...], out_w[0])
        hidden_ref[...] = hidden
        scale = lax.rsqrt(jnp.mean(hidden * hidden, axis=-1, keepdims=True) + epsilon)
        rows = (hidden * scale * narrow_ref[experts + 1 : experts + 2, :].astype(f32)).astype(bf16)
        rows_ref[...] = rows
        router = dot_nt(narrow_ref[:experts, :], rows)
        place = iota((experts, TOK_MB), 0)
        chosen = [
            jnp.sum(jnp.where(ids_ref[k : k + 1, :] == place, router, 0.0), axis=0, keepdims=True)
            for k in range(TOP)
        ]
        gates_ref[0:1, :] = 1.0 / (1.0 + jnp.exp(chosen[1] - chosen[0]))
        gates_ref[1:2, :] = 1.0 / (1.0 + jnp.exp(chosen[0] - chosen[1]))
        size = block_refs[0].shape[0]
        for index, ref in enumerate(block_refs):
            for low in range(0, size, 384):
                hots = [slot_hot(slots_ref[k : k + 1, :], index * size + low, 384) for k in range(TOP)]
                pick = jnp.where(hots[0] | hots[1], 1.0, 0.0).astype(bf16)
                ref[low : low + 384, :] = dot_nn(pick, rows).astype(bf16)


def matrix_specs():
    return [
        pl.BlockSpec((1, D, D), functools.partial(lambda i, h: (i, 0, 0), i), pipeline_mode=pl.Buffered(1))
        for i in range(4)
    ]


def attend(starts, tokens, matrices, narrow, constants, ids, slots, step, blocks, experts, capacity):
    size = experts * capacity // blocks
    fixed = lambda h: (0, 0)
    out_shapes = (
        [((D, TOK_MB), bf16)] * 3
        + [((HEADS, SEQ_LEN, SEQ_LEN), bf16), ((D, TOK_MB), bf16), ((TOK_MB, D), f32), ((TOK_MB, D), bf16)]
        + [((TOP, TOK_MB), f32), ((TOK_MB, D), bf16)]
        + [((size, D), bf16)] * blocks
    )
    out_specs = [
        pl.BlockSpec((1, SEQ_LEN, SEQ_LEN), lambda h: (h, 0, 0)) if len(s) == 3 else resident(s, fixed)
        for s, _ in out_shapes
    ]
    return pl.pallas_call(
        functools.partial(attend_kernel, step=step, experts=experts),
        grid=(HEADS,),
        in_specs=[pl.BlockSpec(memory_space=pltpu.SMEM), resident((TOK_MB, D), lambda h: (step, 0))]
        + matrix_specs()
        + [resident(narrow.shape, fixed)]
        + [resident(c.shape, fixed) for c in constants]
        + [resident((TOP, TOK_MB), lambda h: (0, step)), resident((TOP, TOK_MB), fixed)],
        out_specs=out_specs,
        out_shape=[jax.ShapeDtypeStruct(*s) for s in out_shapes],
        scratch_shapes=[pltpu.VMEM((SEQ_LEN, SEQ_LEN), f32), pltpu.VMEM((16, 1024), f32)],
        compiler_params=pltpu.CompilerParams(vmem_limit_bytes=48 * MIB),
        cost_estimate=lasting(23),
        name="attend",
    )(starts, tokens, *[matrices] * 4, narrow, *constants, ids, slots)


def collect(target, direct, passed, size):
    for index, ref in enumerate(direct):
        low = 2 * index * size
        if passed is None:
            target[...] = ref[...]
        else:
            target[low : low + size, :] = ref[:size, :]
            target[low + size : low + 2 * size, :] = passed[index * size : (index + 1) * size, :]


def expert_kernel(place_ref, *refs, blocks, passes, micro):
    accumulate = micro > 0
    take = blocks + passes
    rows_refs, cot_refs, refs = refs[:take], refs[take : 2 * take], refs[2 * take :]
    other_ref, router_ref, in_ref, out_ref = refs[:4]
    refs = refs[4:]
    if accumulate:
        prior, refs = refs[:5], refs[5:]
    grads, refs = refs[:5], refs[5:]
    result_refs, back_refs = refs[:blocks], refs[blocks : 2 * blocks]
    rows, picks, rows_t, gate_column, result, back, active, inner_grad = refs[2 * blocks :]
    step, me = pl.program_id(0), place_ref[0]
    total, tile = rows.shape[0], ROW_TILE
    senders, capacity = other_ref.shape
    experts = grads[4].shape[0]
    width = capacity if passes else total
    place = iota((experts, width), 0)

    @pl.when(step == 0)
    def _():
        collect(rows, rows_refs[:blocks], rows_refs[blocks] if passes else None, width)
        for index, ref in enumerate(cot_refs[:blocks]):
            low = 2 * index * width if passes else 0
            picks[low : low + width, :] = ref[...]
            if passes:
                first = (MICRO * index + micro) * width
                picks[low + width : low + 2 * width, :] = cot_refs[blocks][first : first + width, :]
        for sender in range(senders):
            here = slice(sender * width, (sender + 1) * width)
            logits = dot_nt(router_ref[:experts, :], rows[here, :])
            other = other_ref[sender : sender + 1, :].astype(jnp.int32)
            own_logit = jnp.sum(jnp.where(place == me, logits, 0.0), axis=0, keepdims=True)
            other_logit = jnp.sum(jnp.where(place == other, logits, 0.0), axis=0, keepdims=True)
            column = row_to_column(1.0 / (1.0 + jnp.exp(other_logit - own_logit)))
            gate_column[here, :] = column
            picks[here, :] = (picks[here, :].astype(f32) * column).astype(bf16)
        for low in range(0, total, tile):
            rows_t[:, low : low + tile] = rows[low : low + tile, :].astype(f32).T.astype(bf16)
        result[...] = jnp.zeros_like(result)
        back[...] = jnp.zeros_like(back)

    def one_tile(index, carry):
        here = pl.ds(pl.multiple_of(index * tile, tile), tile)
        inner = dot_nn(rows[here, :], in_ref[0])
        square = inner * inner
        bend = jnp.tanh(inner * (0.7978845608028654 + 0.035677408136300125 * square))
        half = 0.5 * inner
        low = (half + half * bend).astype(bf16)
        active[here, :] = low
        result[here, :] += dot_nn(low, out_ref[0])
        slope = 0.5 + 0.5 * bend + half * (1.0 - bend * bend) * (0.7978845608028654 + 0.1070322244089004 * square)
        grad = (dot_nt(picks[here, :], out_ref[0]) * slope).astype(bf16)
        inner_grad[here, :] = grad
        back[here, :] += dot_nt(grad, in_ref[0])
        return carry

    lax.fori_loop(0, total // tile, one_tile, 0)

    def store(index, where, value):
        if accumulate:
            value = value + prior[index][where].astype(f32)
        grads[index][where] = value.astype(bf16)

    quarter = D // 4
    for index in range(4):
        first = pl.multiple_of((index ^ place_ref[1]) * quarter, quarter)
        store(index // 2, index % 2, dot_nn(rows_t[pl.ds(first, quarter), :], inner_grad[...]))
    outer = dot_tn(active[...], picks[...])

    @pl.when(step >= 2)
    def _():
        store(2, 0, outer)

    @pl.when(step < 2)
    def _():
        store(3, 0, outer)

    @pl.when(step == pl.num_programs(0) - 1)
    def _():
        router_sum = prior[4][...] if accumulate else jnp.zeros((experts, D), f32)
        for sender in range(senders):
            here = slice(sender * width, (sender + 1) * width)
            low = result[here, :].astype(bf16)
            score = jnp.sum(low.astype(f32) * picks[here, :].astype(f32), axis=-1, keepdims=True)
            choice = column_to_row((1.0 - gate_column[here, :]) * score)
            other = other_ref[sender : sender + 1, :].astype(jnp.int32)
            logit_grad = jnp.where(place == me, choice, 0.0) - jnp.where(place == other, choice, 0.0)
            logit_grad = logit_grad.astype(bf16)
            router_sum = router_sum + dot_nn(logit_grad, rows[here, :])
            total_back = back[here, :] + dot_tn(logit_grad, router_ref[:experts, :])
            index, first = (sender // 2, sender % 2 * width) if passes else (0, 0)
            result_refs[index][first : first + width, :] = low
            back_refs[index][first : first + width, :] = total_back.astype(bf16)
        grads[4][...] = router_sum


def run_expert(place, rows_blocks, cot_blocks, other, narrow, expert_in, expert_out, prior, micro, blocks, experts):
    passes = len(rows_blocks) - blocks
    size = rows_blocks[0].shape[0]
    total = blocks * size
    chunk, quarter = FF // 4, D // 4
    fixed = lambda i, place: (0, 0)
    at = lambda i, place: i ^ 2 ^ place[2]
    weights = [
        pl.BlockSpec((1, D, chunk), lambda i, place: (0, 0, at(i, place))),
        pl.BlockSpec((1, chunk, D), lambda i, place: (0, at(i, place), 0)),
    ]
    grad_specs = [
        pl.BlockSpec((2, quarter, chunk), lambda i, place: (0, 0, at(i, place))),
        pl.BlockSpec((2, quarter, chunk), lambda i, place: (0, 0, at(i, place))),
        pl.BlockSpec((1, chunk, D), lambda i, place: (jnp.maximum(i - 2, 0), 0, 0)),
        pl.BlockSpec((1, chunk, D), lambda i, place: (jnp.minimum(i, 1), 0, 0)),
        resident((experts, D), fixed),
    ]
    grad_shapes = [((2, quarter, FF), bf16)] * 2 + [((2, chunk, D), bf16)] * 2 + [((experts, D), f32)]
    wide = resident((size, D), fixed)
    taken = [wide] * blocks + [resident((blocks * (size // 2), D), fixed)] * passes
    cot_size = size // (1 + passes)
    taken += [resident((cot_size, D), lambda i, place: (micro, 0))] * blocks
    taken += [resident((MICRO * blocks * cot_size, D), fixed)] * passes
    out = pl.pallas_call(
        functools.partial(expert_kernel, blocks=blocks, passes=passes, micro=micro),
        grid_spec=pltpu.PrefetchScalarGridSpec(
            num_scalar_prefetch=1,
            grid=(4,),
            in_specs=taken
            + [resident(other.shape, fixed), resident(narrow.shape, fixed)]
            + weights
            + (grad_specs if prior else []),
            out_specs=grad_specs + [wide] * (2 * blocks),
            scratch_shapes=[
                pltpu.VMEM((total, D), bf16),
                pltpu.VMEM((total, D), bf16),
                pltpu.VMEM((D, total), bf16),
                pltpu.VMEM((total, 1), f32),
                pltpu.VMEM((total, D), f32),
                pltpu.VMEM((total, D), f32),
                pltpu.VMEM((total, chunk), bf16),
                pltpu.VMEM((total, chunk), bf16),
            ],
        ),
        out_shape=[jax.ShapeDtypeStruct(*s) for s in grad_shapes]
        + [jax.ShapeDtypeStruct((size, D), bf16)] * (2 * blocks),
        compiler_params=pltpu.CompilerParams(vmem_limit_bytes=62 * MIB),
        cost_estimate=lasting(62),
        name="expert",
    )(place, *rows_blocks, *cot_blocks, other, narrow, expert_in, expert_out, *(prior or ()))
    return out[:5], out[5 : 5 + blocks], out[5 + blocks :]


def trade(value, groups, mask):
    return lax.ppermute(value, "group", swap(groups, mask))


def add_low(left, right):
    return (left.astype(f32) + right.astype(f32)).astype(bf16)


def first_half(keep, send_away, groups, mask):
    return add_low(keep, trade(send_away, groups, mask))


def second_half(half, groups, mask):
    return half[0], half[1], trade(half[1], groups, mask)


def doubled(kept, _, received, groups, first, second):
    own = add_low(kept, received)
    beside = trade(own, groups, second)
    far = trade(jnp.stack([own, beside]), groups, first)
    return own[None], beside[None], far


def spread_kernel(place_ref, own_ref, beside_ref, far_ref, out_ref, *, code):
    index = pl.program_id(0) ^ place_ref[code]

    @pl.when(index == 0)
    def _():
        out_ref[...] = own_ref[...].astype(f32)

    @pl.when(index == 1)
    def _():
        out_ref[...] = beside_ref[...].astype(f32)

    @pl.when(index > 1)
    def _():
        out_ref[...] = far_ref[...].astype(f32)


def spread_pieces(place, pieces, code):
    shape = pieces[0].shape[1:]
    block = (1, *shape)
    return pl.pallas_call(
        functools.partial(spread_kernel, code=code),
        grid_spec=pltpu.PrefetchScalarGridSpec(
            num_scalar_prefetch=1,
            grid=(4,),
            in_specs=[pl.BlockSpec(block, lambda i, place: (0, 0, 0))] * 2
            + [pl.BlockSpec(block, lambda i, place: ((i ^ place[code]) & 1, 0, 0))],
            out_specs=pl.BlockSpec(block, lambda i, place: (i, 0, 0)),
        ),
        out_shape=jax.ShapeDtypeStruct((4, *shape), f32),
        compiler_params=pltpu.CompilerParams(vmem_limit_bytes=32 * MIB),
        cost_estimate=lasting(6),
        name="spread",
    )(place, *pieces)


def back_kernel(*refs, blocks, passes, experts, devices, final):
    me_ref, refs = refs[0], refs[1:]
    take = blocks + passes
    back_refs, refs = refs[:take], refs[take:]
    (x_ref, cot_ref, query_w, key_w, value_w, out_w, narrow_ref, hot_ref, bucket_ref, heads_ref, slots_ref) = refs[:11]
    (query_ref, key_ref, value_ref, probs_ref, attended_ref, hidden_ref, normed_ref) = refs[11:18]
    refs = refs[18:]
    if final:
        prior, router_grad, refs = refs[: 1 + passes], refs[1 + passes], refs[2 + passes :]
    token_ref, dense_refs, refs = refs[0], refs[1 : 2 + passes], refs[2 + passes :]
    gathered, hidden_grad, out_grad, query_grad, key_grad, value_grad, whole, lines, diagonals = refs
    head = pl.program_id(0)
    total = gathered.shape[0]

    def dense(first, value):
        columns = slice(first, first + value.shape[1])
        if not passes:
            if final:
                value = value + prior[0][:, columns].astype(f32)
            dense_refs[0][:, columns] = value.astype(bf16)
            return
        whole[:, : value.shape[1]] = value
        rows = D // devices
        for k in range(devices):
            start = pl.multiple_of((me_ref[0] ^ k) * rows, 32)
            piece = whole[pl.ds(start, rows), : value.shape[1]]
            here = slice(k // 2 * rows, (k // 2 + 1) * rows)
            if final:
                piece = piece + prior[k % 2][here, columns].astype(f32)
            dense_refs[k % 2][here, columns] = piece.astype(bf16)

    @pl.when(head == 0)
    def _():
        lines[...] = jnp.zeros_like(lines)
        diagonals[...] = jnp.zeros_like(diagonals)
        cot = cot_ref[...].astype(f32)
        collect(gathered, back_refs[:blocks], back_refs[blocks] if passes else None, back_refs[0].shape[0] // 2)
        columns = [row_to_column(slots_ref[k : k + 1, :].astype(f32)).astype(jnp.int32) for k in range(TOP)]
        rows_grad = jnp.zeros((TOK_MB, D), f32)
        for low in range(0, total, 512):
            place = iota((TOK_MB, 512), 1) + low
            pick = jnp.where((place == columns[0]) | (place == columns[1]), 1.0, 0.0).astype(bf16)
            rows_grad = rows_grad + dot_nn(pick, gathered[low : low + 512, :])
        hidden = hidden_ref[...]
        scale = lax.rsqrt(jnp.mean(hidden * hidden, axis=-1, keepdims=True) + epsilon)
        normal = hidden * scale
        lines[experts + 1 : experts + 2, :] = jnp.sum(rows_grad * normal, axis=0, keepdims=True)
        scaled = rows_grad * narrow_ref[experts + 1 : experts + 2, :].astype(f32)
        total_grad = cot + scale * (scaled - normal * jnp.mean(scaled * normal, axis=-1, keepdims=True))
        hidden_grad[...] = total_grad
        branch = total_grad.astype(bf16)
        dense(3 * D, dot_nn(attended_ref[...], branch))
        out_grad[...] = dot_nt(out_w[0], branch).astype(bf16)

    span = pl.ds(pl.multiple_of(head * HEAD_DIM, HEAD_DIM), HEAD_DIM)
    low = probs_ref[0]
    grad_here = out_grad[span, :]
    probs = low.astype(f32)
    value_grad[span, :] = dot_nt(grad_here, low).astype(bf16)
    prob_grad = dot_tn(value_ref[span, :], grad_here)
    center = jnp.sum(probs * prob_grad, axis=0, keepdims=True)
    score_grad = (probs * (prob_grad - center)).astype(bf16)
    query_grad[span, :] = (dot_nn(key_ref[span, :], score_grad) * HEAD_DIM**-0.5).astype(bf16)
    key_grad[span, :] = dot_nt(query_ref[span, :], score_grad).astype(bf16)
    wide = score_grad.astype(f32)
    pieces = []
    for a in range(4):
        piece = wide[a * 128 : a * 128 + 128, :]
        left, right = 384 - a * 128, 128 + a * 128
        ends = [jnp.zeros((128, left), f32)] if left else []
        pieces.append(jnp.concatenate(ends + [piece, jnp.zeros((128, right), f32)], axis=1))
    folded = pieces[0] + pieces[1] + pieces[2] + pieces[3]
    for half in (64, 32, 16, 8):
        folded = folded[:half] + pltpu.roll(folded[half:], 1024 - half, 1)
    low_row = iota((8, 1024), 0)
    for bit in (4, 2, 1):
        folded = jnp.where((low_row & bit) != 0, pltpu.roll(folded, 1024 - bit, 1), folded)
    diagonals[pl.ds(head, 1), :] = jnp.sum(folded, axis=0, keepdims=True)

    @pl.when(head == HEADS - 1)
    def _():
        normed_t = normed_ref[...].astype(f32).T.astype(bf16)
        grads = (query_grad[...], key_grad[...], value_grad[...])
        in_grad = jnp.zeros((D, TOK_MB), f32)
        for i, (grad, weight) in enumerate(zip(grads, (query_w, key_w, value_w))):
            dense(i * D, dot_nt(normed_t, grad))
            in_grad = in_grad + dot_nn(weight[0], grad)
        in_grad = in_grad.T
        x = x_ref[...].astype(f32)
        scale = lax.rsqrt(jnp.mean(x * x, axis=-1, keepdims=True) + epsilon)
        normal = x * scale
        lines[experts : experts + 1, :] = jnp.sum(in_grad * normal, axis=0, keepdims=True)
        scaled = in_grad * narrow_ref[experts : experts + 1, :].astype(f32)
        grad = hidden_grad[...] + scale * (scaled - normal * jnp.mean(scaled * normal, axis=-1, keepdims=True))
        token_ref[...] = grad.astype(bf16)
        if final:
            lines[:experts, :] = router_grad[...]
        by_bucket = sum_dot(diagonals[...], hot_ref[...], dot_nt)
        by_place = sum_dot(by_bucket, bucket_ref[...], dot_nt)
        lines[experts + 2 : experts + 3, :] = jnp.sum(by_place * heads_ref[...].astype(f32), axis=0, keepdims=True)
        dense(4 * D, lines[...].T)


def sum_dot(values, hot, dot):
    high = values.astype(bf16)
    return dot(high, hot) + dot((values - high.astype(f32)).astype(bf16), hot)


def backward(me, back_blocks, tokens, cotangent, matrices, narrow, constants, slots, saved, prior, step, blocks, experts, devices):
    passes = len(back_blocks) - blocks
    size = back_blocks[0].shape[0]
    fixed = lambda h: (0, 0)
    block = lambda h: (step, 0)
    head_block = pl.BlockSpec((1, SEQ_LEN, SEQ_LEN), lambda h: (h, 0, 0))
    wide = 4 * D + 128
    dense_shapes = [(D // (1 + passes), wide)] * (1 + passes)
    dense_specs = [resident(s, fixed) for s in dense_shapes]
    return pl.pallas_call(
        functools.partial(
            back_kernel, blocks=blocks, passes=passes, experts=experts, devices=devices, final=prior is not None
        ),
        grid=(HEADS,),
        in_specs=[pl.BlockSpec(memory_space=pltpu.SMEM)]
        + [resident(b.shape, fixed) for b in back_blocks]
        + [resident((TOK_MB, D), block)] * 2
        + matrix_specs()
        + [resident(narrow.shape, fixed)]
        + [resident(c.shape, fixed) for c in constants]
        + [resident((TOP, TOK_MB), fixed)]
        + [head_block if s.ndim == 3 else resident(s.shape, fixed) for s in saved]
        + (dense_specs + [resident((experts, D), fixed)] if prior else []),
        out_specs=[resident((TOK_MB, D), fixed)] + dense_specs,
        out_shape=[jax.ShapeDtypeStruct((TOK_MB, D), bf16)] + [jax.ShapeDtypeStruct(s, bf16) for s in dense_shapes],
        scratch_shapes=[
            pltpu.VMEM((blocks * size, D), bf16),
            pltpu.VMEM((TOK_MB, D), f32),
            pltpu.VMEM((D, TOK_MB), bf16),
            pltpu.VMEM((D, TOK_MB), bf16),
            pltpu.VMEM((D, TOK_MB), bf16),
            pltpu.VMEM((D, TOK_MB), bf16),
            pltpu.VMEM((D, D), f32),
            pltpu.VMEM((128, D), f32),
            pltpu.VMEM((16, 1024), f32),
        ],
        compiler_params=pltpu.CompilerParams(vmem_limit_bytes=58 * MIB),
        cost_estimate=lasting(34),
        name="backward",
    )(me, *back_blocks, tokens, cotangent, *[matrices] * 4, narrow, *constants, slots, *saved, *(prior or ()))


def combine_kernel(*refs, blocks, passes):
    result_refs = refs[: blocks + passes]
    hidden_ref, slots_ref, gates_ref, mixed_ref, gathered = refs[blocks + passes :]
    collect(gathered, result_refs[:blocks], result_refs[blocks] if passes else None, result_refs[0].shape[0] // 2)
    slots = [row_to_column(slots_ref[k : k + 1, :].astype(f32)).astype(jnp.int32) for k in range(TOP)]
    gates = [row_to_column(gates_ref[k : k + 1, :]) for k in range(TOP)]
    output = hidden_ref[...]
    for k in range(TOP):
        picked = jnp.zeros((TOK_MB, D), f32)
        for low in range(0, gathered.shape[0], 512):
            pick = jnp.where(iota((TOK_MB, 512), 1) + low == slots[k], 1.0, 0.0).astype(bf16)
            picked = picked + dot_nn(pick, gathered[low : low + 512, :])
        output = output + gates[k] * picked
    mixed_ref[...] = output.astype(bf16)


def combine(result_blocks, hidden, slots, gates, blocks):
    total = blocks * result_blocks[0].shape[0]
    return pl.pallas_call(
        functools.partial(combine_kernel, blocks=blocks, passes=len(result_blocks) - blocks),
        out_shape=jax.ShapeDtypeStruct((TOK_MB, D), bf16),
        scratch_shapes=[pltpu.VMEM((total, D), bf16)],
        compiler_params=pltpu.CompilerParams(vmem_limit_bytes=32 * MIB),
        cost_estimate=lasting(3),
        name="combine",
    )(*result_blocks, hidden, slots, gates)


def tie(values, *after):
    count = len(values)
    return list(lax.optimization_barrier((*values, *after)))[:count]


def send(blocks, devices):
    if len(blocks) == 1:
        whole = blocks[0]
        moved = whole.reshape(devices, -1, D)
        moved = lax.all_to_all(moved, "expert", split_axis=0, concat_axis=0, tiled=True)
        return [moved.reshape(whole.shape)]
    return [blocks[0]] + [
        lax.ppermute(blocks[j], "expert", swap(devices, 2 * j)) for j in range(1, len(blocks))
    ]


def pass_on(blocks, devices):
    if len(blocks) == 1:
        return blocks
    half = blocks[0].shape[0] // 2
    second = jnp.concatenate([b[half:] for b in blocks], axis=0)
    return [*blocks, lax.ppermute(second, "expert", swap(devices, 1))]


def reduce_dense(pieces, devices):
    if len(pieces) == 1:
        return lax.psum_scatter(pieces[0], "expert", scatter_dimension=0, tiled=True).astype(f32)
    near, cross = pieces
    chips = devices // 2
    rows = near.shape[0] // chips
    summed = near.astype(f32) + lax.ppermute(cross, "expert", swap(devices, 1)).astype(f32)
    low = summed.astype(bf16)
    total = summed[:rows]
    for j in range(1, chips):
        total = total + lax.ppermute(low[j * rows : (j + 1) * rows], "expert", swap(devices, 2 * j)).astype(f32)
    return total


def reduce_group(total, groups):
    mask = 1
    while mask < groups:
        low = total.astype(bf16)
        total = low.astype(f32) + lax.ppermute(low, "group", swap(groups, mask)).astype(f32)
        mask *= 2
    return total


def shards(
    tokens, cotangent, norm_attn, w_query, w_key, w_value, w_out, rel_bias, norm_expert, w_router,
    expert_in, expert_out, expert_ids, span_starts,
):
    experts = w_router.shape[1]
    capacity = 3 * TOK_MB * TOP // (2 * experts)
    groups, devices = lax.axis_size("group"), lax.axis_size("expert")
    direct = devices <= DIRECT_MAX
    blocks = devices // 2 if direct else 1
    shard, share = w_query.shape[0], rel_bias.shape[0]
    me = lax.axis_index("expert").reshape(1).astype(jnp.int32)
    order = me if direct else jnp.zeros_like(me)
    ids = expert_ids.T
    group = lax.axis_index("group").reshape(1).astype(jnp.int32)
    place = jnp.concatenate([me, group % 2 * 2 + group // 2, group])

    padded = jnp.pad(rel_bias, (0, shard - share))
    narrow = jnp.concatenate([w_router.T, norm_attn[None], norm_expert[None], padded[None]], axis=0)
    matrices, narrow, all_ids = gather_weights(
        (w_query, w_key, w_value, w_out), narrow, ids, groups, devices
    )
    bucket, heads = bias_places(devices)
    constants = (bucket_hot().astype(bf16), bucket.astype(bf16), heads.astype(bf16))

    slots, *cots = route(order, ids, cotangent, blocks, experts, capacity)
    if not direct:
        cots = cots[0].reshape(MICRO, devices, capacity, D).transpose(1, 0, 2, 3).reshape(-1, D)
        cots = send([cots], devices)[0].reshape(devices, MICRO, capacity, D).transpose(1, 0, 2, 3).reshape(-1, D)
        cots = [cots]
    else:
        cots = send(cots, devices)
    other = partners(me, all_ids, devices, capacity, direct)
    if not direct:
        other = other.reshape(MICRO, 1, devices * capacity)
    saved, sent = [], []
    for step in range(MICRO):
        out = attend(
            span_starts, tokens, matrices, narrow, constants, ids, slots[step], step, blocks, experts, capacity
        )
        saved.append(out[:9])
        sent.append(out[9:])
    cots = tie(cots, saved[0][0], saved[1][0])
    sent[0] = send(tie(sent[0], *cots[1:]), devices)
    sent[1] = send(tie(sent[1], *sent[0][1:]), devices)
    cots = pass_on(cots, devices)
    sent[0] = pass_on(sent[0], devices)

    grads, result, back = run_expert(
        place, sent[0], cots, other[0], narrow, expert_in, expert_out, None, 0, blocks, experts
    )
    sent[1] = pass_on(tie(sent[1], back[0]), devices)
    backs, results = [send(back, devices)], [result]
    grads, result, back = run_expert(
        place, sent[1], cots, other[1], narrow, expert_in, expert_out, grads, 1, blocks, experts
    )
    results.append(result)
    inward = first_half(grads[0], grads[1], groups, 1)
    outward = first_half(grads[2], grads[3], groups, 2)
    backs[0] = pass_on(tie(backs[0], back[0]), devices)
    backs.append(send(tie(back, *backs[0]), devices))

    def run_back(step, prior):
        query, key, value, probs, attended, hidden, _, _, normed = saved[step]
        return backward(
            order, backs[step], tokens, cotangent, matrices, narrow, constants, slots[step],
            (query, key, value, probs, attended, hidden, normed), prior, step, blocks, experts, devices,
        )

    token_grads = [None, None]
    token_grads[0], *dense = run_back(0, None)
    backs[1] = pass_on(tie(backs[1], token_grads[0]), devices)
    results[0] = send(tie(results[0], *backs[1]), devices)
    backs[1] = tie(backs[1], inward, outward)
    inward = second_half(inward, groups, 2)
    outward = second_half(outward, groups, 1)
    token_grads[1], *dense = run_back(1, (*dense, grads[4]))
    results[0] = tie(results[0], token_grads[1])
    total = reduce_dense(tie(dense, *results[0][1:]), devices)
    results[1] = send(tie(results[1], total), devices)
    inward = doubled(*inward, groups, 1, 2)
    outward = doubled(*outward, groups, 2, 1)
    total = reduce_group(total, groups)
    mixed = [
        combine(pass_on(results[step], devices), saved[step][5], slots[step], saved[step][7], blocks)
        for step in range(MICRO)
    ]
    thin = total[:, 4 * D :]
    grad_in = spread_pieces(place, inward, 1).reshape(expert_in.shape)
    grad_out = spread_pieces(place, outward, 2).reshape(expert_out.shape)
    return (
        jnp.concatenate(mixed, axis=0),
        jnp.concatenate(token_grads, axis=0),
        thin[:, experts],
        total[:, :D],
        total[:, D : 2 * D],
        total[:, 2 * D : 3 * D],
        total[:, 3 * D : 4 * D],
        thin[:share, experts + 2],
        thin[:, experts + 1],
        thin[:, :experts],
        grad_in,
        grad_out,
    )


def solution(mesh):
    rows, split = P(("group", "expert"), None), P("expert", None)
    stacked = P("expert", None, None)
    return jax.shard_map(
        shards,
        mesh=mesh,
        in_specs=(
            rows, rows, P("expert"), split, split, split, split, P("expert"), P("expert"), split,
            stacked, stacked, rows, P(("group", "expert")),
        ),
        out_specs=(
            rows, rows, P("expert"), split, split, split, split, P("expert"), P("expert"), split, stacked, stacked,
        ),
        check_vma=False,
    )
```

```python
import functools

import jax
import jax.numpy as jnp
import numpy as np
from jax import lax
from jax.experimental import pallas as pl
from jax.experimental.pallas import tpu as pltpu
from jax.sharding import PartitionSpec as P

D = 768
HEADS = 12
HEAD_DIM = 64
FF = 3072
TOP = 2
BUCKETS = 32
SEQ_LEN = 512
PIC = 256
MICRO = 2
TOK_MB = 512
ROW_TILE = 256
DIRECT_MAX = 8
COST_BYTES = 3600000

epsilon = 1e-06
bucket_edges = (1, 2, 3, 4, 5, 6, 7, 8, 12, 16, 23, 32, 45, 64, 91)
f32 = jnp.float32
bf16 = jnp.bfloat16
MIB = 1 << 20


def dot_nn(left, right):
    return lax.dot_general(left, right, (((1,), (0,)), ((), ())), preferred_element_type=f32)


def dot_nt(left, right):
    return lax.dot_general(left, right, (((1,), (1,)), ((), ())), preferred_element_type=f32)


def dot_tn(left, right):
    return lax.dot_general(left, right, (((0,), (0,)), ((), ())), preferred_element_type=f32)


def iota(shape, dim):
    return lax.broadcasted_iota(jnp.int32, shape, dim)


def diagonal_offsets():
    place = np.arange(1024)
    return np.where(place < 896, 384 - place, 1408 - place)


def bucket_hot():
    offset = diagonal_offsets()
    magnitude = sum((np.abs(offset) >= edge).astype(np.int32) for edge in bucket_edges)
    bucket = magnitude + 16 * (offset > 0)
    hot = bucket[None, :] == np.arange(BUCKETS)[:, None]
    return hot & (np.abs(offset) < SEQ_LEN)[None, :]


def lasting(microseconds):
    return pl.CostEstimate(flops=0, bytes_accessed=int(microseconds * COST_BYTES), transcendentals=0)


def resident(shape, index):
    return pl.BlockSpec(shape, index, pipeline_mode=pl.Buffered(1))


def split_rows(values):
    high = values.astype(bf16).astype(f32)
    row = iota((8, values.shape[1]), 0)
    return jnp.where(row == 0, high, jnp.where(row == 1, values - high, 0.0)).astype(bf16)


def row_to_column(row):
    size = row.shape[1]
    step = 128 if size % 128 == 0 else size
    eye = iota((step, step), 0) == iota((step, step), 1)
    columns = [
        jnp.sum(jnp.where(eye, row[:, i : i + step], 0.0), axis=1, keepdims=True)
        for i in range(0, size, step)
    ]
    return columns[0] if len(columns) == 1 else jnp.concatenate(columns, axis=0)


def column_to_row(column):
    size = column.shape[0]
    step = 128 if size % 128 == 0 else size
    eye = iota((step, step), 0) == iota((step, step), 1)
    rows = [
        jnp.sum(jnp.where(eye, column[i : i + step], 0.0), axis=0, keepdims=True)
        for i in range(0, size, step)
    ]
    return rows[0] if len(rows) == 1 else jnp.concatenate(rows, axis=1)


def slot_hot(slot_row, first, size):
    return iota((size, TOK_MB), 0) + first == slot_row


def route_kernel(me_ref, ids_ref, cot_ref, slots_ref, *block_refs, experts, capacity):
    place = iota((experts, TOK_MB), 0)
    earlier = earlier_places()
    for step in range(MICRO):
        here = slice(step * TOK_MB, (step + 1) * TOK_MB)
        hots = [ids_ref[k : k + 1, here] == place for k in range(TOP)]
        both = jnp.where(hots[0] | hots[1], 1.0, 0.0).astype(bf16)
        at = dot_nn(both, earlier) + ((place ^ me_ref[0]) * capacity).astype(f32)
        slots = [jnp.sum(jnp.where(hot, at, 0.0), axis=0, keepdims=True).astype(jnp.int32) for hot in hots]
        for k in range(TOP):
            slots_ref[step, k : k + 1, :] = slots[k]
        blocks = block_refs[step * len(block_refs) // MICRO : (step + 1) * len(block_refs) // MICRO]
        size = blocks[0].shape[0]
        for first in range(0, experts * capacity, 384):
            hot = slot_hot(slots[0], first, 384) | slot_hot(slots[1], first, 384)
            value = dot_nn(jnp.where(hot, 1.0, 0.0).astype(bf16), cot_ref[here, :]).astype(bf16)
            blocks[first // size][first % size : first % size + 384, :] = value


def earlier_places():
    return jnp.where(iota((TOK_MB, TOK_MB), 0) < iota((TOK_MB, TOK_MB), 1), 1.0, 0.0).astype(bf16)


def route(me, ids, cotangent, blocks, experts, capacity):
    size = experts * capacity // blocks
    slots, *out = pl.pallas_call(
        functools.partial(route_kernel, experts=experts, capacity=capacity),
        in_specs=[pl.BlockSpec(memory_space=pltpu.SMEM)] + [pl.BlockSpec(memory_space=pltpu.VMEM)] * 2,
        out_shape=[jax.ShapeDtypeStruct((MICRO, TOP, TOK_MB), jnp.int32)]
        + [jax.ShapeDtypeStruct((size, D), bf16)] * (MICRO * blocks),
        compiler_params=pltpu.CompilerParams(vmem_limit_bytes=32 * MIB),
        cost_estimate=lasting(4),
        name="route",
    )(me, ids, cotangent)
    return slots, [out[step * blocks : (step + 1) * blocks] for step in range(MICRO)]


def partner_kernel(me_ref, ids_ref, other_ref, *, xor):
    devices, capacity = other_ref.shape[1:]
    earlier = earlier_places()
    mine = me_ref[0].astype(f32)
    for step in range(MICRO):
        first, second = ids_ref[step], ids_ref[MICRO + step]
        hot = (first == mine) | (second == mine)
        order = dot_nn(jnp.where(hot, 1.0, 0.0).astype(bf16), earlier).astype(jnp.int32)
        order = jnp.where(hot, order, -1)
        partner = (first + second - mine).astype(bf16)
        for sender in range(devices):
            pick = jnp.where(iota((capacity, TOK_MB), 0) == order[sender : sender + 1, :], 1.0, 0.0).astype(bf16)
            found = dot_nt(partner, pick)[sender : sender + 1, :]
            row = sender ^ me_ref[0] if xor else sender
            other_ref[step, pl.ds(row, 1), :] = found


def partners(me, ids, devices, capacity, xor):
    return pl.pallas_call(
        functools.partial(partner_kernel, xor=xor),
        in_specs=[pl.BlockSpec(memory_space=pltpu.SMEM)] + [pl.BlockSpec(memory_space=pltpu.VMEM)],
        out_shape=jax.ShapeDtypeStruct((MICRO, devices, capacity), f32),
        compiler_params=pltpu.CompilerParams(vmem_limit_bytes=32 * MIB),
        cost_estimate=lasting(1.3),
        name="partners",
    )(me, ids)


def unpack_kernel(place_ref, *refs, groups, chips, lines):
    own, (passed, *smalls, out_ref, narrow_ref, ids_ref) = refs[:groups], refs[groups:]
    rows = own[0].shape[0] // chips
    me = place_ref[1]
    for k in range(groups):
        for j in range(chips):
            low = (k * chips + j) * rows
            values = own[k][j * rows : (j + 1) * rows, :], passed[low : low + rows, :]
            for core in range(2):
                here = pl.ds(pl.multiple_of((me ^ (2 * j + core)) * rows, rows), rows)
                out_ref[place_ref[0] ^ k, here, :] = values[core]
    gathered = jnp.zeros((16, D), f32)
    lane = iota((16, D), 1)
    for k in range(2 * chips):
        block = smalls[k % 2][k // 2 * 16 : k // 2 * 16 + 16, :].astype(f32)
        device = me ^ k
        gathered = gathered + pltpu.roll(jnp.where(lane < rows, block, 0.0), device * rows, 1)
        for pick in range(TOP * MICRO):
            ids_ref[pick, pl.ds(device, 1), :] = block[lines + pick : lines + pick + 1, :TOK_MB]
    narrow_ref[...] = gathered.astype(bf16)


def gather_weights(matrices, narrow, ids, blocks, groups, devices):
    lines, shard = narrow.shape
    if devices > DIRECT_MAX:
        whole = jnp.stack([lax.all_gather(w, "expert", axis=0, tiled=True) for w in matrices])
        flat = jnp.concatenate([narrow.reshape(-1), ids.astype(bf16).reshape(-1)])
        flat = lax.all_gather(flat, "expert", axis=0)
        narrow = flat[:, : lines * shard].reshape(devices, lines, shard).transpose(1, 0, 2).reshape(lines, D)
        ids = flat[:, lines * shard :].astype(f32).reshape(devices, TOP * MICRO, TOK_MB).transpose(1, 0, 2)
        return whole, narrow, ids, send(blocks, devices)
    chips = devices // 2
    group, me = lax.axis_index("group"), lax.axis_index("expert")
    mine = matrices[0]
    for index in range(1, groups):
        mine = jnp.where(group == index, matrices[index], mine)
    small = jnp.concatenate(
        [
            jnp.pad(narrow, ((0, 0), (0, D - shard))),
            jnp.pad(ids.astype(bf16).reshape(TOP * MICRO, TOK_MB), ((0, 0), (0, D - TOK_MB))),
            jnp.zeros((16 - lines - TOP * MICRO, D), bf16),
        ],
        axis=0,
    )
    mine = jnp.concatenate([mine, small], axis=0)
    mine = [mine] + [lax.ppermute(mine, "expert", swap(devices, 2 * j)) for j in range(1, chips)]
    small = jnp.concatenate([m[shard:] for m in mine], axis=0)
    mine = jnp.concatenate([m[:shard] for m in mine], axis=0)
    blocks = send(tie(blocks, mine), devices)
    near = lax.ppermute(mine, "group", swap(groups, 1))
    far = lax.ppermute(mine, "group", swap(groups, 2))
    near, far = tie([near, far], blocks[chips // 2])
    half = mine.shape[0] // 2
    low = lax.ppermute(far[:half], "group", swap(groups, 1))
    high = lax.ppermute(near[half:], "group", swap(groups, 2))
    own = [mine, near, far, jnp.concatenate([low, high], axis=0)]
    (passed,) = tie([jnp.concatenate(own, axis=0)], *blocks[1:])
    passed = lax.ppermute(passed, "expert", swap(devices, 1))
    passed_small = lax.ppermute(small, "expert", swap(devices, 1))
    place = jnp.stack([group, me]).astype(jnp.int32)
    whole, narrow, ids = pl.pallas_call(
        functools.partial(unpack_kernel, groups=groups, chips=chips, lines=lines),
        in_specs=[pl.BlockSpec(memory_space=pltpu.SMEM)] + [pl.BlockSpec(memory_space=pltpu.VMEM)] * (groups + 3),
        out_shape=[
            jax.ShapeDtypeStruct((groups, D, D), bf16),
            jax.ShapeDtypeStruct((16, D), bf16),
            jax.ShapeDtypeStruct((TOP * MICRO, devices, TOK_MB), f32),
        ],
        compiler_params=pltpu.CompilerParams(vmem_limit_bytes=32 * MIB),
        cost_estimate=lasting(3),
        name="unpack",
    )(place, *own, passed, small, passed_small)
    return whole, narrow, ids, blocks


def swap(devices, mask):
    return [(i, i ^ mask) for i in range(devices)]


def bias_places(devices):
    place = np.arange(D)
    wide, share = D // devices, HEADS * BUCKETS // devices
    flat = place // wide * share + place % wide
    used = place % wide < share
    bucket = (flat[:, None] % BUCKETS == np.arange(BUCKETS)[None, :]) & used[:, None]
    head = (flat[None, :] // BUCKETS == np.arange(16)[:, None]) & used[None, :]
    return bucket.astype(np.float32), head.astype(np.float32)


def attend_kernel(
    starts_ref, x_ref, query_w, key_w, value_w, out_w, narrow_ref, hot_ref, bucket_ref, heads_ref, ids_ref, slots_ref,
    query_ref, key_ref, value_ref, probs_ref, attended_ref, hidden_ref, rows_ref, gates_ref, normed_ref,
    *refs, step, experts,
):
    block_refs, (mask_ref, table_ref) = refs[:-2], refs[-2:]
    head = pl.program_id(0)

    @pl.when(head == 0)
    def _():
        x = x_ref[...].astype(f32)
        scale = lax.rsqrt(jnp.mean(x * x, axis=-1, keepdims=True) + epsilon)
        normed = (x * scale * narrow_ref[experts : experts + 1, :].astype(f32)).astype(bf16)
        normed_ref[...] = normed
        query = dot_nn(normed, query_w[0]).astype(bf16).astype(f32) * HEAD_DIM**-0.5
        query_ref[...] = query.T.astype(bf16)
        key_ref[...] = dot_nn(normed, key_w[0]).T.astype(bf16)
        value_ref[...] = dot_nn(normed, value_w[0]).T.astype(bf16)
        rel = (heads_ref[...].astype(f32) * narrow_ref[experts + 2 : experts + 3, :].astype(f32)).astype(bf16)
        table_ref[...] = dot_nn(dot_nn(rel, bucket_ref[...]).astype(bf16), hot_ref[...])
        start = starts_ref[step]
        key_place, query_place = iota((SEQ_LEN, SEQ_LEN), 0), iota((SEQ_LEN, SEQ_LEN), 1)
        inside = (
            (key_place >= start)
            & (key_place < start + PIC)
            & (query_place >= start)
            & (query_place < start + PIC)
        )
        mask_ref[...] = jnp.where((key_place <= query_place) | inside, 0.0, -1e30)

    span = pl.ds(pl.multiple_of(head * HEAD_DIM, HEAD_DIM), HEAD_DIM)
    table = jnp.broadcast_to(table_ref[pl.ds(head, 1), :], (8, 1024))
    low_row = iota((8, 1024), 0)
    for bit in (1, 2, 4):
        table = jnp.where((low_row & bit) != 0, pltpu.roll(table, bit, 1), table)
    for shift in (8, 16, 32, 64):
        table = jnp.concatenate([table, pltpu.roll(table, shift, 1)], axis=0)
    scores = dot_tn(key_ref[span, :], query_ref[span, :])
    bias = jnp.concatenate([table[:, 384 - a * 128 : 896 - a * 128] for a in range(4)], axis=0)
    scores = scores + bias + mask_ref[...]
    expo = jnp.exp(scores - jnp.max(scores, axis=0, keepdims=True))
    probs = (expo * (1.0 / jnp.sum(expo, axis=0, keepdims=True))).astype(bf16)
    probs_ref[0] = probs
    attended_ref[span, :] = dot_nn(value_ref[span, :], probs).astype(bf16)

    @pl.when(head == HEADS - 1)
    def _():
        hidden = x_ref[...].astype(f32) + dot_tn(attended_ref[...], out_w[0])
        hidden_ref[...] = hidden
        scale = lax.rsqrt(jnp.mean(hidden * hidden, axis=-1, keepdims=True) + epsilon)
        rows = (hidden * scale * narrow_ref[experts + 1 : experts + 2, :].astype(f32)).astype(bf16)
        rows_ref[...] = rows
        router = dot_nt(narrow_ref[:experts, :], rows)
        place = iota((experts, TOK_MB), 0)
        chosen = [
            jnp.sum(jnp.where(ids_ref[k : k + 1, :] == place, router, 0.0), axis=0, keepdims=True)
            for k in range(TOP)
        ]
        gates_ref[0:1, :] = 1.0 / (1.0 + jnp.exp(chosen[1] - chosen[0]))
        gates_ref[1:2, :] = 1.0 / (1.0 + jnp.exp(chosen[0] - chosen[1]))
        half = block_refs[0].shape[0] // (4 // len(block_refs))
        for first in range(0, 4 * half, half):
            hots = [slot_hot(slots_ref[k : k + 1, :], first, half) for k in range(TOP)]
            value = dot_nn(jnp.where(hots[0] | hots[1], 1.0, 0.0).astype(bf16), rows).astype(bf16)
            low = first // 2
            if len(block_refs) == 1:
                block_refs[0][first : first + half, :] = value
            else:
                block_refs[0][low : low + half // 2, :] = value[: half // 2]
                block_refs[1][low : low + half // 2, :] = value[half // 2 :]


def matrix_specs():
    return [
        pl.BlockSpec((1, D, D), functools.partial(lambda i, h: (i, 0, 0), i), pipeline_mode=pl.Buffered(1))
        for i in range(4)
    ]


def attend(starts, tokens, matrices, narrow, constants, ids, slots, step, direct, experts, capacity):
    size = experts * capacity // (1 + direct)
    fixed = lambda h: (0, 0)
    out_shapes = (
        [((D, TOK_MB), bf16)] * 3
        + [((HEADS, SEQ_LEN, SEQ_LEN), bf16), ((D, TOK_MB), bf16), ((TOK_MB, D), f32), ((TOK_MB, D), bf16)]
        + [((TOP, TOK_MB), f32), ((TOK_MB, D), bf16)]
        + [((size, D), bf16)] * (1 + direct)
    )
    out_specs = [
        pl.BlockSpec((1, SEQ_LEN, SEQ_LEN), lambda h: (h, 0, 0)) if len(s) == 3 else resident(s, fixed)
        for s, _ in out_shapes
    ]
    return pl.pallas_call(
        functools.partial(attend_kernel, step=step, experts=experts),
        grid=(HEADS,),
        in_specs=[pl.BlockSpec(memory_space=pltpu.SMEM), resident((TOK_MB, D), lambda h: (step, 0))]
        + matrix_specs()
        + [resident(narrow.shape, fixed)]
        + [resident(c.shape, fixed) for c in constants]
        + [resident((TOP, TOK_MB), lambda h: (0, step)), resident((TOP, TOK_MB), fixed)],
        out_specs=out_specs,
        out_shape=[jax.ShapeDtypeStruct(*s) for s in out_shapes],
        scratch_shapes=[pltpu.VMEM((SEQ_LEN, SEQ_LEN), f32), pltpu.VMEM((16, 1024), f32)],
        compiler_params=pltpu.CompilerParams(vmem_limit_bytes=48 * MIB),
        cost_estimate=lasting(23),
        name="attend",
    )(starts, tokens, *[matrices] * 4, narrow, *constants, ids, slots)


def collect(target, direct, passed, size):
    if passed is None:
        for index, ref in enumerate(direct):
            target[index * ref.shape[0] : (index + 1) * ref.shape[0], :] = ref[...]
        return
    for index, ref in enumerate(direct):
        low = 2 * index * size
        target[low : low + size, :] = ref[...]
        target[low + size : low + 2 * size, :] = passed[index * size : (index + 1) * size, :]


def received_specs(received, blocks, size):
    first = lambda *_: (0, 0)
    return [resident((size, D), first)] * blocks + [resident(r.shape, first) for r in received[blocks:]]


def expert_kernel(place_ref, *refs, blocks, passes, micro):
    accumulate = micro > 0
    rows_refs, cot_refs, refs = refs[:blocks], refs[blocks : 2 * blocks + passes], refs[2 * blocks + passes :]
    other_ref, router_ref, in_ref, out_ref = refs[:4]
    refs = refs[4:]
    if accumulate:
        prior, refs = refs[:5], refs[5:]
    grads, refs = refs[:5], refs[5:]
    result_refs, back_refs = refs[:blocks], refs[blocks : 2 * blocks]
    rows, picks, rows_t, gate_column, result, back, active, inner_grad = refs[2 * blocks :]
    step, me = pl.program_id(0), place_ref[0]
    total, tile = rows.shape[0], ROW_TILE
    senders, capacity = other_ref.shape
    experts = grads[4].shape[0]
    width = capacity if passes else total
    place = iota((experts, width), 0)

    @pl.when(step == 0)
    def _():
        collect(rows, rows_refs, None, width)
        collect(picks, cot_refs[:blocks], cot_refs[blocks] if passes else None, width)
        for sender in range(senders):
            here = slice(sender * width, (sender + 1) * width)
            logits = dot_nt(router_ref[:experts, :], rows[here, :])
            other = other_ref[sender : sender + 1, :].astype(jnp.int32)
            own_logit = jnp.sum(jnp.where(place == me, logits, 0.0), axis=0, keepdims=True)
            other_logit = jnp.sum(jnp.where(place == other, logits, 0.0), axis=0, keepdims=True)
            column = row_to_column(1.0 / (1.0 + jnp.exp(other_logit - own_logit)))
            gate_column[here, :] = column
            picks[here, :] = (picks[here, :].astype(f32) * column).astype(bf16)
        for low in range(0, total, tile):
            rows_t[:, low : low + tile] = rows[low : low + tile, :].astype(f32).T.astype(bf16)
        result[...] = jnp.zeros_like(result)
        back[...] = jnp.zeros_like(back)

    def one_tile(index):
        here = slice(index * tile, (index + 1) * tile)
        inner = dot_nn(rows[here, :], in_ref[0])
        square = inner * inner
        bend = jnp.tanh(inner * (0.7978845608028654 + 0.035677408136300125 * square))
        half = 0.5 * inner
        low = (half + half * bend).astype(bf16)
        active[here, :] = low
        result[here, :] += dot_nn(low, out_ref[0])
        slope = 0.5 + 0.5 * bend + half * (1.0 - bend * bend) * (0.7978845608028654 + 0.1070322244089004 * square)
        grad = (dot_nt(picks[here, :], out_ref[0]) * slope).astype(bf16)
        inner_grad[here, :] = grad
        back[here, :] += dot_nt(grad, in_ref[0])

    for index in range(total // tile):
        one_tile(index)

    def store(index, where, value):
        if accumulate:
            value = value + prior[index][where].astype(f32)
        grads[index][where] = value.astype(bf16)

    quarter = D // 4
    for index in range(4):
        first = pl.multiple_of((index ^ place_ref[1]) * quarter, quarter)
        store(index // 2, index % 2, dot_nn(rows_t[pl.ds(first, quarter), :], inner_grad[...]))
    outer = dot_tn(active[...], picks[...])

    @pl.when(step >= 2)
    def _():
        store(2, 0, outer)

    @pl.when(step < 2)
    def _():
        store(3, 0, outer)

    @pl.when(step == pl.num_programs(0) - 1)
    def _():
        router_sum = prior[4][...] if accumulate else jnp.zeros((experts, D), f32)
        for sender in range(senders):
            here = slice(sender * width, (sender + 1) * width)
            low = result[here, :].astype(bf16)
            score = jnp.sum(low.astype(f32) * picks[here, :].astype(f32), axis=-1, keepdims=True)
            choice = column_to_row((1.0 - gate_column[here, :]) * score)
            other = other_ref[sender : sender + 1, :].astype(jnp.int32)
            logit_grad = jnp.where(place == me, choice, 0.0) - jnp.where(place == other, choice, 0.0)
            logit_grad = logit_grad.astype(bf16)
            router_sum = router_sum + dot_nn(logit_grad, rows[here, :])
            total_back = back[here, :] + dot_tn(logit_grad, router_ref[:experts, :])
            index, first = (sender // 2, sender % 2 * width) if passes else (0, 0)
            back_refs[index][first : first + width, :] = total_back.astype(bf16)
            result_refs[index][first : first + width, :] = low
        grads[4][...] = router_sum


def run_expert(place, rows_blocks, cot_blocks, other, narrow, expert_in, expert_out, prior, micro, blocks, experts):
    passes = len(cot_blocks) - blocks
    size = rows_blocks[0].shape[0]
    total = blocks * size
    fixed = lambda i, place: (0, 0)
    chunk, quarter = FF // 4, D // 4
    at = lambda i, place: i ^ 2 ^ place[2]
    weights = [
        pl.BlockSpec((1, D, chunk), lambda i, place: (0, 0, at(i, place))),
        pl.BlockSpec((1, chunk, D), lambda i, place: (0, at(i, place), 0)),
    ]
    grad_specs = [
        pl.BlockSpec((2, quarter, chunk), lambda i, place: (0, 0, at(i, place))),
        pl.BlockSpec((2, quarter, chunk), lambda i, place: (0, 0, at(i, place))),
        pl.BlockSpec((1, chunk, D), lambda i, place: (jnp.maximum(i - 2, 0), 0, 0)),
        pl.BlockSpec((1, chunk, D), lambda i, place: (jnp.minimum(i, 1), 0, 0)),
        resident((experts, D), fixed),
    ]
    grad_shapes = [((2, quarter, FF), bf16)] * 2 + [((2, chunk, D), bf16)] * 2 + [((experts, D), f32)]
    taken = received_specs(rows_blocks, blocks, size)
    taken += received_specs(cot_blocks, blocks, size // (1 + passes))
    out = pl.pallas_call(
        functools.partial(expert_kernel, blocks=blocks, passes=passes, micro=micro),
        grid_spec=pltpu.PrefetchScalarGridSpec(
            num_scalar_prefetch=1,
            grid=(4,),
            in_specs=taken
            + [resident(other.shape, fixed), resident(narrow.shape, fixed)]
            + weights
            + (grad_specs if prior else []),
            out_specs=grad_specs + [resident((size, D), fixed)] * (2 * blocks),
            scratch_shapes=[
                pltpu.VMEM((total, D), bf16),
                pltpu.VMEM((total, D), bf16),
                pltpu.VMEM((D, total), bf16),
                pltpu.VMEM((total, 1), f32),
                pltpu.VMEM((total, D), f32),
                pltpu.VMEM((total, D), f32),
                pltpu.VMEM((total, chunk), bf16),
                pltpu.VMEM((total, chunk), bf16),
            ],
        ),
        out_shape=[jax.ShapeDtypeStruct(*s) for s in grad_shapes]
        + [jax.ShapeDtypeStruct((size, D), bf16)] * (2 * blocks),
        compiler_params=pltpu.CompilerParams(vmem_limit_bytes=62 * MIB),
        cost_estimate=lasting(62),
        name="expert",
    )(place, *rows_blocks, *cot_blocks, other, narrow, expert_in, expert_out, *(prior or ()))
    return out[:5], out[5:]


def trade(value, groups, mask):
    return lax.ppermute(value, "group", swap(groups, mask))


def add_low(left, right):
    return (left.astype(f32) + right.astype(f32)).astype(bf16)


def second_half(half, groups, mask):
    return add_low(half[0], trade(half[1], groups, mask))


def spread_kernel(place_ref, own_ref, beside_ref, far_ref, out_ref, *, code):
    index = pl.program_id(0) ^ place_ref[code]

    @pl.when(index == 0)
    def _():
        out_ref[...] = own_ref[...].astype(f32)

    @pl.when(index == 1)
    def _():
        out_ref[...] = beside_ref[...].astype(f32)

    @pl.when(index > 1)
    def _():
        out_ref[...] = far_ref[...].astype(f32)


def spread_pieces(place, pieces, code):
    shape = pieces[0].shape[1:]
    block = (1, *shape)
    return pl.pallas_call(
        functools.partial(spread_kernel, code=code),
        grid_spec=pltpu.PrefetchScalarGridSpec(
            num_scalar_prefetch=1,
            grid=(4,),
            in_specs=[pl.BlockSpec(block, lambda i, place: (0, 0, 0))] * 2
            + [pl.BlockSpec(block, lambda i, place: ((i ^ place[code]) & 1, 0, 0))],
            out_specs=pl.BlockSpec(block, lambda i, place: (i, 0, 0)),
        ),
        out_shape=jax.ShapeDtypeStruct((4, *shape), f32),
        compiler_params=pltpu.CompilerParams(vmem_limit_bytes=32 * MIB),
        cost_estimate=lasting(6),
        name="spread",
    )(place, *pieces)


def back_kernel(*refs, blocks, passes, experts, devices, final):
    me_ref, refs = refs[0], refs[1:]
    take = blocks + passes
    back_refs, refs = refs[:take], refs[take:]
    (x_ref, cot_ref, query_w, key_w, value_w, out_w, narrow_ref, hot_ref, bucket_ref, heads_ref, slots_ref) = refs[:11]
    (query_ref, key_ref, value_ref, probs_ref, attended_ref, hidden_ref, normed_ref) = refs[11:18]
    refs = refs[18:]
    if final:
        prior, router_grad, refs = refs[: 1 + passes], refs[1 + passes], refs[2 + passes :]
    token_ref, dense_refs, refs = refs[0], refs[1 : 2 + passes], refs[2 + passes :]
    gathered, hidden_grad, out_grad, query_grad, key_grad, value_grad, whole, lines, diagonals = refs
    head = pl.program_id(0)
    total = gathered.shape[0]

    def dense(first, value):
        columns = slice(first, first + value.shape[1])
        if not passes:
            if final:
                value = value + prior[0][:, columns].astype(f32)
            dense_refs[0][:, columns] = value.astype(bf16)
            return
        whole[:, : value.shape[1]] = value
        rows = D // devices
        for k in range(devices):
            start = pl.multiple_of((me_ref[0] ^ k) * rows, 32)
            piece = whole[pl.ds(start, rows), : value.shape[1]]
            here = slice(k // 2 * rows, (k // 2 + 1) * rows)
            if final:
                piece = piece + prior[k % 2][here, columns].astype(f32)
            dense_refs[k % 2][here, columns] = piece.astype(bf16)

    @pl.when(head == 0)
    def _():
        lines[...] = jnp.zeros_like(lines)
        diagonals[...] = jnp.zeros_like(diagonals)
        cot = cot_ref[...].astype(f32)
        collect(gathered, back_refs[:blocks], back_refs[blocks] if passes else None, back_refs[0].shape[0])
        columns = [row_to_column(slots_ref[k : k + 1, :].astype(f32)).astype(jnp.int32) for k in range(TOP)]
        rows_grad = jnp.zeros((TOK_MB, D), f32)
        for low in range(0, total, 512):
            place = iota((TOK_MB, 512), 1) + low
            pick = jnp.where((place == columns[0]) | (place == columns[1]), 1.0, 0.0).astype(bf16)
            rows_grad = rows_grad + dot_nn(pick, gathered[low : low + 512, :])
        hidden = hidden_ref[...]
        scale = lax.rsqrt(jnp.mean(hidden * hidden, axis=-1, keepdims=True) + epsilon)
        normal = hidden * scale
        lines[experts + 1 : experts + 2, :] = jnp.sum(rows_grad * normal, axis=0, keepdims=True)
        scaled = rows_grad * narrow_ref[experts + 1 : experts + 2, :].astype(f32)
        total_grad = cot + scale * (scaled - normal * jnp.mean(scaled * normal, axis=-1, keepdims=True))
        hidden_grad[...] = total_grad
        branch = total_grad.astype(bf16)
        dense(3 * D, dot_nn(attended_ref[...], branch))
        out_grad[...] = dot_nt(out_w[0], branch).astype(bf16)

    span = pl.ds(pl.multiple_of(head * HEAD_DIM, HEAD_DIM), HEAD_DIM)
    low = probs_ref[0]
    grad_here = out_grad[span, :]
    probs = low.astype(f32)
    value_grad[span, :] = dot_nt(grad_here, low).astype(bf16)
    prob_grad = dot_tn(value_ref[span, :], grad_here)
    center = jnp.sum(probs * prob_grad, axis=0, keepdims=True)
    score_grad = (probs * (prob_grad - center)).astype(bf16)
    query_grad[span, :] = (dot_nn(key_ref[span, :], score_grad) * HEAD_DIM**-0.5).astype(bf16)
    key_grad[span, :] = dot_nt(query_ref[span, :], score_grad).astype(bf16)
    wide = score_grad.astype(f32)
    pieces = []
    for a in range(4):
        piece = wide[a * 128 : a * 128 + 128, :]
        left, right = 384 - a * 128, 128 + a * 128
        ends = [jnp.zeros((128, left), f32)] if left else []
        pieces.append(jnp.concatenate(ends + [piece, jnp.zeros((128, right), f32)], axis=1))
    folded = pieces[0] + pieces[1] + pieces[2] + pieces[3]
    for half in (64, 32, 16, 8):
        folded = folded[:half] + pltpu.roll(folded[half:], 1024 - half, 1)
    low_row = iota((8, 1024), 0)
    for bit in (4, 2, 1):
        folded = jnp.where((low_row & bit) != 0, pltpu.roll(folded, 1024 - bit, 1), folded)
    diagonals[pl.ds(head, 1), :] = jnp.sum(folded, axis=0, keepdims=True)

    @pl.when(head == HEADS - 1)
    def _():
        normed_t = normed_ref[...].astype(f32).T.astype(bf16)
        grads = (query_grad[...], key_grad[...], value_grad[...])
        in_grad = jnp.zeros((D, TOK_MB), f32)
        for i, (grad, weight) in enumerate(zip(grads, (query_w, key_w, value_w))):
            dense(i * D, dot_nt(normed_t, grad))
            in_grad = in_grad + dot_nn(weight[0], grad)
        in_grad = in_grad.T
        x = x_ref[...].astype(f32)
        scale = lax.rsqrt(jnp.mean(x * x, axis=-1, keepdims=True) + epsilon)
        normal = x * scale
        lines[experts : experts + 1, :] = jnp.sum(in_grad * normal, axis=0, keepdims=True)
        scaled = in_grad * narrow_ref[experts : experts + 1, :].astype(f32)
        grad = hidden_grad[...] + scale * (scaled - normal * jnp.mean(scaled * normal, axis=-1, keepdims=True))
        token_ref[...] = grad.astype(bf16)
        if final:
            lines[:experts, :] = router_grad[...]
        by_bucket = sum_dot(diagonals[...], hot_ref[...], dot_nt)
        by_place = sum_dot(by_bucket, bucket_ref[...], dot_nt)
        lines[experts + 2 : experts + 3, :] = jnp.sum(by_place * heads_ref[...].astype(f32), axis=0, keepdims=True)
        dense(4 * D, lines[...].T)


def sum_dot(values, hot, dot):
    high = values.astype(bf16)
    return dot(high, hot) + dot((values - high.astype(f32)).astype(bf16), hot)


def backward(me, back_blocks, tokens, cotangent, matrices, narrow, constants, slots, saved, prior, step, blocks, experts, devices, slot_count):
    passes = len(back_blocks) - blocks
    size = slot_count // blocks // (1 + passes)
    fixed = lambda h: (0, 0)
    block = lambda h: (step, 0)
    head_block = pl.BlockSpec((1, SEQ_LEN, SEQ_LEN), lambda h: (h, 0, 0))
    wide = 4 * D + 128
    dense_shapes = [(D // (1 + passes), wide)] * (1 + passes)
    dense_specs = [resident(s, fixed) for s in dense_shapes]
    return pl.pallas_call(
        functools.partial(
            back_kernel, blocks=blocks, passes=passes, experts=experts, devices=devices, final=prior is not None
        ),
        grid=(HEADS,),
        in_specs=[pl.BlockSpec(memory_space=pltpu.SMEM)]
        + received_specs(back_blocks, blocks, size)
        + [resident((TOK_MB, D), block)] * 2
        + matrix_specs()
        + [resident(narrow.shape, fixed)]
        + [resident(c.shape, fixed) for c in constants]
        + [resident((TOP, TOK_MB), fixed)]
        + [head_block if s.ndim == 3 else resident(s.shape, fixed) for s in saved]
        + (dense_specs + [resident((experts, D), fixed)] if prior else []),
        out_specs=[resident((TOK_MB, D), fixed)] + dense_specs,
        out_shape=[jax.ShapeDtypeStruct((TOK_MB, D), bf16)] + [jax.ShapeDtypeStruct(s, bf16) for s in dense_shapes],
        scratch_shapes=[
            pltpu.VMEM((slot_count, D), bf16),
            pltpu.VMEM((TOK_MB, D), f32),
            pltpu.VMEM((D, TOK_MB), bf16),
            pltpu.VMEM((D, TOK_MB), bf16),
            pltpu.VMEM((D, TOK_MB), bf16),
            pltpu.VMEM((D, TOK_MB), bf16),
            pltpu.VMEM((D, D), f32),
            pltpu.VMEM((128, D), f32),
            pltpu.VMEM((16, 1024), f32),
        ],
        compiler_params=pltpu.CompilerParams(vmem_limit_bytes=58 * MIB),
        cost_estimate=lasting(34),
        name="backward",
    )(me, *back_blocks, tokens, cotangent, *[matrices] * 4, narrow, *constants, slots, *saved, *(prior or ()))


def combine_kernel(*refs, blocks, passes):
    result_refs = refs[: blocks + passes]
    hidden_ref, slots_ref, gates_ref, mixed_ref, gathered = refs[blocks + passes :]
    size = result_refs[0].shape[0]
    collect(gathered, result_refs[:blocks], result_refs[blocks] if passes else None, size)
    slots = [row_to_column(slots_ref[k : k + 1, :].astype(f32)).astype(jnp.int32) for k in range(TOP)]
    gates = [row_to_column(gates_ref[k : k + 1, :]) for k in range(TOP)]
    output = hidden_ref[...]
    for k in range(TOP):
        picked = jnp.zeros((TOK_MB, D), f32)
        for low in range(0, gathered.shape[0], 512):
            pick = jnp.where(iota((TOK_MB, 512), 1) + low == slots[k], 1.0, 0.0).astype(bf16)
            picked = picked + dot_nn(pick, gathered[low : low + 512, :])
        output = output + gates[k] * picked
    mixed_ref[...] = output.astype(bf16)


def combine(received, hidden, slots, gates, blocks, slot_count):
    passes = len(received) - blocks
    size = slot_count // blocks // (1 + passes)
    fixed = lambda i: (0, 0)
    return pl.pallas_call(
        functools.partial(combine_kernel, blocks=blocks, passes=passes),
        grid=(1,),
        in_specs=received_specs(received, blocks, size)
        + [resident(a.shape, fixed) for a in (hidden, slots, gates)],
        out_specs=resident((TOK_MB, D), fixed),
        out_shape=jax.ShapeDtypeStruct((TOK_MB, D), bf16),
        scratch_shapes=[pltpu.VMEM((slot_count, D), bf16)],
        compiler_params=pltpu.CompilerParams(vmem_limit_bytes=32 * MIB),
        cost_estimate=lasting(3),
        name="combine",
    )(*received, hidden, slots, gates)


def tie(values, *after):
    count = len(values)
    return list(lax.optimization_barrier((*values, *after)))[:count]


def send(blocks, devices):
    if len(blocks) == 1:
        whole = blocks[0]
        moved = whole.reshape(devices, -1, D)
        moved = lax.all_to_all(moved, "expert", split_axis=0, concat_axis=0, tiled=True)
        return [moved.reshape(whole.shape)]
    return [blocks[0]] + [
        lax.ppermute(blocks[j], "expert", swap(devices, 2 * j)) for j in range(1, len(blocks))
    ]


def pair_up(near, cross, devices):
    got = lax.ppermute(cross, "expert", swap(devices, 1))
    size = 2 * near.shape[0] // devices
    return [jnp.concatenate([a[low : low + size] for a in (near, got)]) for low in range(0, near.shape[0], size)]


def pass_on(blocks, devices):
    if len(blocks) == 1:
        return blocks
    half = blocks[0].shape[0] // 2
    second = jnp.concatenate([b[half:] for b in blocks], axis=0)
    return [*blocks, lax.ppermute(second, "expert", swap(devices, 1))]


def sum_cores(pieces, devices):
    near, cross = pieces
    return near.astype(f32) + lax.ppermute(cross, "expert", swap(devices, 1)).astype(f32)


def sum_chips(own, low, devices):
    chips = devices // 2
    rows = low.shape[0] // chips
    for j in range(1, chips):
        own = own + lax.ppermute(low[j * rows : (j + 1) * rows], "expert", swap(devices, 2 * j)).astype(f32)
    return own


def reduce_group(total, groups, *after):
    mask = 1
    while mask < groups:
        low = total.astype(bf16)
        if mask > 1:
            (low,) = tie([low], *after)
        total = low.astype(f32) + lax.ppermute(low, "group", swap(groups, mask)).astype(f32)
        mask *= 2
    return total


def shards(
    tokens, cotangent, norm_attn, w_query, w_key, w_value, w_out, rel_bias, norm_expert, w_router,
    expert_in, expert_out, expert_ids, span_starts,
):
    experts = w_router.shape[1]
    capacity = 3 * TOK_MB * TOP // (2 * experts)
    groups, devices = lax.axis_size("group"), lax.axis_size("expert")
    direct = devices <= DIRECT_MAX
    blocks = devices // 2 if direct else 1
    shard, share = w_query.shape[0], rel_bias.shape[0]
    me = lax.axis_index("expert").reshape(1).astype(jnp.int32)
    order = me if direct else jnp.zeros_like(me)
    ids = expert_ids.T
    group = lax.axis_index("group").reshape(1).astype(jnp.int32)
    place = jnp.concatenate([me, group % 2 * 2 + group // 2, group])

    padded = jnp.pad(rel_bias, (0, shard - share))
    narrow = jnp.concatenate([w_router.T, norm_attn[None], norm_expert[None], padded[None]], axis=0)
    slots, cots = route(order, ids, cotangent, blocks, experts, capacity)
    matrices, narrow, all_ids, cots[0] = gather_weights(
        (w_query, w_key, w_value, w_out), narrow, ids, cots[0], groups, devices
    )
    bucket, heads = bias_places(devices)
    constants = (bucket_hot().astype(bf16), bucket.astype(bf16), heads.astype(bf16))
    slot_count = experts * capacity
    cots[1] = send(tie(cots[1], *cots[0][1:]), devices)
    other = partners(me, all_ids, devices, capacity, direct)
    if not direct:
        other = other.reshape(MICRO, 1, slot_count)
    (narrow,) = tie([narrow], *cots[0][1:], other)
    saved, sent = [], []
    for step in range(MICRO):
        out = attend(
            span_starts, tokens, matrices, narrow, constants, ids, slots[step], step, direct, experts, capacity
        )
        saved.append(out[:9])
        sent.append(out[9:])
    cots[1] = tie(cots[1], saved[0][0], saved[1][0])
    if direct:
        sent = [pair_up(*tie(s, *cots[1][1:]), devices) for s in sent]
    sent[0] = send(tie(sent[0], *cots[1][1:]), devices)
    cots = [pass_on(tie(c, saved[1][0]), devices) for c in cots]
    sent[1] = send(tie(sent[1], *sent[0][1:]), devices)

    grads, first = run_expert(
        place, sent[0], cots[0], other[0], narrow, expert_in, expert_out, None, 0, blocks, experts
    )
    sent[1] = tie(sent[1], first[0])
    results, backs = [first[:blocks]], [send(tie(first[blocks:], *sent[1]), devices)]
    grads, last = run_expert(
        place, sent[1], cots[1], other[1], narrow, expert_in, expert_out, grads, 1, blocks, experts
    )
    results.append(last[:blocks])
    backs.append(last[blocks:])
    *flat, router_grad = tie(grads, *backs[0][1:])
    away = [trade(flat[1], groups, 1), trade(flat[3], groups, 2)]
    backs[0] = pass_on(tie(backs[0], last[0]), devices)
    backs[1] = send(tie(backs[1], *backs[0]), devices)

    def run_back(step, prior):
        query, key, value, probs, attended, hidden, _, _, normed = saved[step]
        return backward(
            order, backs[step], tokens, cotangent, matrices, narrow, constants, slots[step],
            (query, key, value, probs, attended, hidden, normed), prior, step, blocks, experts, devices, slot_count,
        )

    token_grads = [None, None]
    token_grads[0], *dense = run_back(0, None)
    backs[1] = pass_on(tie(backs[1], token_grads[0]), devices)
    away = tie(away, *backs[1])
    halves = [add_low(flat[0], away[0]), add_low(flat[2], away[1])]
    owns = [second_half(halves[0], groups, 2), second_half(halves[1], groups, 1)]
    if direct:
        results[0] = send(tie(results[0], *backs[1]), devices)
    else:
        results = [send(r, devices) for r in results]
    backs[1] = tie(backs[1], *halves)
    token_grads[1], *dense = run_back(1, (*dense, router_grad))
    owns = tie(owns, token_grads[1], *results[0])
    if direct:
        results[0] = pass_on(tie(results[0], token_grads[1]), devices)
    if direct:
        dense = tie(dense, *results[0][1:-1], *owns)
        total = sum_cores(dense, devices)
        low = total.astype(bf16)
        owns = tie(owns, low)
    besides = [trade(owns[0], groups, 2), trade(owns[1], groups, 1)]
    fars = [jnp.stack(pair) for pair in zip(owns, besides)]
    if direct:
        total = sum_chips(total[:shard], low, devices)
        results[1] = send(tie(results[1], total), devices)
        (total,) = tie([total], results[1][1])
        results[1] = pass_on(results[1], devices)
    else:
        total = lax.psum_scatter(dense[0], "expert", scatter_dimension=0, tiled=True).astype(f32)
    fars = [trade(fars[0], groups, 1), trade(fars[1], groups, 2)]
    inward, outward = [(own[None], beside[None], far) for own, beside, far in zip(owns, besides, fars)]
    mixed = [
        combine(results[step], saved[step][5], slots[step], saved[step][7], blocks, slot_count)
        for step in range(MICRO)
    ]
    (total,) = tie([total], mixed[0])
    grad_in = spread_pieces(place, inward, 1).reshape(expert_in.shape)
    grad_out = spread_pieces(place, outward, 2).reshape(expert_out.shape)
    total = reduce_group(total, groups, grad_in, grad_out)
    thin = total[:, 4 * D :]
    return (
        jnp.concatenate(mixed, axis=0),
        jnp.concatenate(token_grads, axis=0),
        thin[:, experts],
        total[:, :D],
        total[:, D : 2 * D],
        total[:, 2 * D : 3 * D],
        total[:, 3 * D : 4 * D],
        thin[:share, experts + 2],
        thin[:, experts + 1],
        thin[:, :experts],
        grad_in,
        grad_out,
    )


def solution(mesh):
    rows, split = P(("group", "expert"), None), P("expert", None)
    stacked = P("expert", None, None)
    return jax.shard_map(
        shards,
        mesh=mesh,
        in_specs=(
            rows, rows, P("expert"), split, split, split, split, P("expert"), P("expert"), split,
            stacked, stacked, rows, P(("group", "expert")),
        ),
        out_specs=(
            rows, rows, P("expert"), split, split, split, split, P("expert"), P("expert"), split, stacked, stacked,
        ),
        check_vma=False,
    )
```

```python
import functools

import jax
import jax.numpy as jnp
import numpy as np
from jax import lax
from jax.experimental import pallas as pl
from jax.experimental.pallas import tpu as pltpu
from jax.sharding import PartitionSpec as P

D = 768
HEADS = 12
HEAD_DIM = 64
FF = 3072
TOP = 2
BUCKETS = 32
SEQ_LEN = 512
PIC = 256
MICRO = 2
TOK_MB = 512
ROW_TILE = 256
DIRECT_MAX = 8
COST_BYTES = 3600000

epsilon = 1e-06
bucket_edges = (1, 2, 3, 4, 5, 6, 7, 8, 12, 16, 23, 32, 45, 64, 91)
f32 = jnp.float32
bf16 = jnp.bfloat16
MIB = 1 << 20


def dot_nn(left, right):
    return lax.dot_general(left, right, (((1,), (0,)), ((), ())), preferred_element_type=f32)


def dot_nt(left, right):
    return lax.dot_general(left, right, (((1,), (1,)), ((), ())), preferred_element_type=f32)


def dot_tn(left, right):
    return lax.dot_general(left, right, (((0,), (0,)), ((), ())), preferred_element_type=f32)


def iota(shape, dim):
    return lax.broadcasted_iota(jnp.int32, shape, dim)


def diagonal_offsets():
    place = np.arange(1024)
    return np.where(place < 896, 384 - place, 1408 - place)


def bucket_hot():
    offset = diagonal_offsets()
    magnitude = sum((np.abs(offset) >= edge).astype(np.int32) for edge in bucket_edges)
    bucket = magnitude + 16 * (offset > 0)
    hot = bucket[None, :] == np.arange(BUCKETS)[:, None]
    return hot & (np.abs(offset) < SEQ_LEN)[None, :]


def lasting(microseconds):
    return pl.CostEstimate(flops=0, bytes_accessed=int(microseconds * COST_BYTES), transcendentals=0)


def resident(shape, index):
    return pl.BlockSpec(shape, index, pipeline_mode=pl.Buffered(1))


def split_rows(values):
    high = values.astype(bf16).astype(f32)
    row = iota((8, values.shape[1]), 0)
    return jnp.where(row == 0, high, jnp.where(row == 1, values - high, 0.0)).astype(bf16)


def row_to_column(row):
    size = row.shape[1]
    step = 128 if size % 128 == 0 else size
    eye = iota((step, step), 0) == iota((step, step), 1)
    columns = [
        jnp.sum(jnp.where(eye, row[:, i : i + step], 0.0), axis=1, keepdims=True)
        for i in range(0, size, step)
    ]
    return columns[0] if len(columns) == 1 else jnp.concatenate(columns, axis=0)


def column_to_row(column):
    size = column.shape[0]
    step = 128 if size % 128 == 0 else size
    eye = iota((step, step), 0) == iota((step, step), 1)
    rows = [
        jnp.sum(jnp.where(eye, column[i : i + step], 0.0), axis=0, keepdims=True)
        for i in range(0, size, step)
    ]
    return rows[0] if len(rows) == 1 else jnp.concatenate(rows, axis=1)


def slot_hot(slot_row, first, size):
    return iota((size, TOK_MB), 0) + first == slot_row


def route_kernel(me_ref, ids_ref, cot_ref, slots_ref, *block_refs, experts, capacity):
    place = iota((experts, TOK_MB), 0)
    earlier = earlier_places()
    for step in range(MICRO):
        here = slice(step * TOK_MB, (step + 1) * TOK_MB)
        hots = [ids_ref[k : k + 1, here] == place for k in range(TOP)]
        both = jnp.where(hots[0] | hots[1], 1.0, 0.0).astype(bf16)
        at = dot_nn(both, earlier) + ((place ^ me_ref[0]) * capacity).astype(f32)
        slots = [jnp.sum(jnp.where(hot, at, 0.0), axis=0, keepdims=True).astype(jnp.int32) for hot in hots]
        for k in range(TOP):
            slots_ref[step, k : k + 1, :] = slots[k]
        blocks = block_refs[step * len(block_refs) // MICRO : (step + 1) * len(block_refs) // MICRO]
        size = blocks[0].shape[0]
        for first in range(0, experts * capacity, 384):
            hot = slot_hot(slots[0], first, 384) | slot_hot(slots[1], first, 384)
            value = dot_nn(jnp.where(hot, 1.0, 0.0).astype(bf16), cot_ref[here, :]).astype(bf16)
            blocks[first // size][first % size : first % size + 384, :] = value


def earlier_places():
    return jnp.where(iota((TOK_MB, TOK_MB), 0) < iota((TOK_MB, TOK_MB), 1), 1.0, 0.0).astype(bf16)


def route(me, ids, cotangent, blocks, experts, capacity):
    size = experts * capacity // blocks
    slots, *out = pl.pallas_call(
        functools.partial(route_kernel, experts=experts, capacity=capacity),
        in_specs=[pl.BlockSpec(memory_space=pltpu.SMEM)] + [pl.BlockSpec(memory_space=pltpu.VMEM)] * 2,
        out_shape=[jax.ShapeDtypeStruct((MICRO, TOP, TOK_MB), jnp.int32)]
        + [jax.ShapeDtypeStruct((size, D), bf16)] * (MICRO * blocks),
        compiler_params=pltpu.CompilerParams(vmem_limit_bytes=32 * MIB),
        cost_estimate=lasting(4),
        name="route",
    )(me, ids, cotangent)
    return slots, [out[step * blocks : (step + 1) * blocks] for step in range(MICRO)]


def partner_kernel(me_ref, ids_ref, other_ref, *, xor):
    devices, capacity = other_ref.shape[1:]
    earlier = earlier_places()
    mine = me_ref[0].astype(f32)
    for step in range(MICRO):
        first, second = ids_ref[step], ids_ref[MICRO + step]
        hot = (first == mine) | (second == mine)
        order = dot_nn(jnp.where(hot, 1.0, 0.0).astype(bf16), earlier).astype(jnp.int32)
        order = jnp.where(hot, order, -1)
        partner = (first + second - mine).astype(bf16)
        for sender in range(devices):
            pick = jnp.where(iota((capacity, TOK_MB), 0) == order[sender : sender + 1, :], 1.0, 0.0).astype(bf16)
            found = dot_nt(partner, pick)[sender : sender + 1, :]
            row = sender ^ me_ref[0] if xor else sender
            other_ref[step, pl.ds(row, 1), :] = found


def partners(me, ids, devices, capacity, xor):
    return pl.pallas_call(
        functools.partial(partner_kernel, xor=xor),
        in_specs=[pl.BlockSpec(memory_space=pltpu.SMEM)] + [pl.BlockSpec(memory_space=pltpu.VMEM)],
        out_shape=jax.ShapeDtypeStruct((MICRO, devices, capacity), f32),
        compiler_params=pltpu.CompilerParams(vmem_limit_bytes=32 * MIB),
        cost_estimate=lasting(1.3),
        name="partners",
    )(me, ids)


def unpack_kernel(place_ref, *refs, groups, chips, lines):
    own, (passed, *smalls, out_ref, narrow_ref, ids_ref) = refs[:groups], refs[groups:]
    rows = own[0].shape[0] // chips
    me = place_ref[1]
    for k in range(groups):
        for j in range(chips):
            low = (k * chips + j) * rows
            values = own[k][j * rows : (j + 1) * rows, :], passed[low : low + rows, :]
            for core in range(2):
                here = pl.ds(pl.multiple_of((me ^ (2 * j + core)) * rows, rows), rows)
                out_ref[place_ref[0] ^ k, here, :] = values[core]
    gathered = jnp.zeros((16, D), f32)
    lane = iota((16, D), 1)
    for k in range(2 * chips):
        block = smalls[k % 2][k // 2 * 16 : k // 2 * 16 + 16, :].astype(f32)
        device = me ^ k
        gathered = gathered + pltpu.roll(jnp.where(lane < rows, block, 0.0), device * rows, 1)
        for pick in range(TOP * MICRO):
            ids_ref[pick, pl.ds(device, 1), :] = block[lines + pick : lines + pick + 1, :TOK_MB]
    narrow_ref[...] = gathered.astype(bf16)


def gather_weights(matrices, narrow, ids, blocks, groups, devices):
    lines, shard = narrow.shape
    if devices > DIRECT_MAX:
        whole = jnp.stack([lax.all_gather(w, "expert", axis=0, tiled=True) for w in matrices])
        flat = jnp.concatenate([narrow.reshape(-1), ids.astype(bf16).reshape(-1)])
        flat = lax.all_gather(flat, "expert", axis=0)
        narrow = flat[:, : lines * shard].reshape(devices, lines, shard).transpose(1, 0, 2).reshape(lines, D)
        ids = flat[:, lines * shard :].astype(f32).reshape(devices, TOP * MICRO, TOK_MB).transpose(1, 0, 2)
        return whole, narrow, ids, send(blocks, devices)
    chips = devices // 2
    group, me = lax.axis_index("group"), lax.axis_index("expert")
    mine = matrices[0]
    for index in range(1, groups):
        mine = jnp.where(group == index, matrices[index], mine)
    small = jnp.concatenate(
        [
            jnp.pad(narrow, ((0, 0), (0, D - shard))),
            jnp.pad(ids.astype(bf16).reshape(TOP * MICRO, TOK_MB), ((0, 0), (0, D - TOK_MB))),
            jnp.zeros((16 - lines - TOP * MICRO, D), bf16),
        ],
        axis=0,
    )
    mine = jnp.concatenate([mine, small], axis=0)
    mine = [mine] + [lax.ppermute(mine, "expert", swap(devices, 2 * j)) for j in range(1, chips)]
    small = jnp.concatenate([m[shard:] for m in mine], axis=0)
    mine = jnp.concatenate([m[:shard] for m in mine], axis=0)
    blocks = send(tie(blocks, mine), devices)
    near = lax.ppermute(mine, "group", swap(groups, 1))
    far = lax.ppermute(mine, "group", swap(groups, 2))
    near, far = tie([near, far], blocks[chips // 2])
    half = mine.shape[0] // 2
    low = lax.ppermute(far[:half], "group", swap(groups, 1))
    high = lax.ppermute(near[half:], "group", swap(groups, 2))
    own = [mine, near, far, jnp.concatenate([low, high], axis=0)]
    (passed,) = tie([jnp.concatenate(own, axis=0)], *blocks[1:])
    passed = lax.ppermute(passed, "expert", swap(devices, 1))
    passed_small = lax.ppermute(small, "expert", swap(devices, 1))
    place = jnp.stack([group, me]).astype(jnp.int32)
    whole, narrow, ids = pl.pallas_call(
        functools.partial(unpack_kernel, groups=groups, chips=chips, lines=lines),
        in_specs=[pl.BlockSpec(memory_space=pltpu.SMEM)] + [pl.BlockSpec(memory_space=pltpu.VMEM)] * (groups + 3),
        out_shape=[
            jax.ShapeDtypeStruct((groups, D, D), bf16),
            jax.ShapeDtypeStruct((16, D), bf16),
            jax.ShapeDtypeStruct((TOP * MICRO, devices, TOK_MB), f32),
        ],
        compiler_params=pltpu.CompilerParams(vmem_limit_bytes=32 * MIB),
        cost_estimate=lasting(3),
        name="unpack",
    )(place, *own, passed, small, passed_small)
    return whole, narrow, ids, blocks


def swap(devices, mask):
    return [(i, i ^ mask) for i in range(devices)]


def bias_places(devices):
    place = np.arange(D)
    wide, share = D // devices, HEADS * BUCKETS // devices
    flat = place // wide * share + place % wide
    used = place % wide < share
    bucket = (flat[:, None] % BUCKETS == np.arange(BUCKETS)[None, :]) & used[:, None]
    head = (flat[None, :] // BUCKETS == np.arange(16)[:, None]) & used[None, :]
    return bucket.astype(np.float32), head.astype(np.float32)


def attend_kernel(
    starts_ref, x_ref, query_w, key_w, value_w, out_w, narrow_ref, hot_ref, bucket_ref, heads_ref, ids_ref, slots_ref,
    query_ref, key_ref, value_ref, probs_ref, attended_ref, hidden_ref, gates_ref, normed_ref,
    *refs, experts,
):
    block_refs, (mask_ref, table_ref) = refs[:-2], refs[-2:]
    head = pl.program_id(0)
    spans = [slice(step * TOK_MB, (step + 1) * TOK_MB) for step in range(MICRO)]

    @pl.when(head == 0)
    def _():
        x = x_ref[...].astype(f32)
        scale = lax.rsqrt(jnp.mean(x * x, axis=-1, keepdims=True) + epsilon)
        normed = (x * scale * narrow_ref[experts : experts + 1, :].astype(f32)).astype(bf16)
        query = dot_nn(normed, query_w[0]).astype(bf16).astype(f32) * HEAD_DIM**-0.5
        key, value = dot_nn(normed, key_w[0]), dot_nn(normed, value_w[0])
        key_place, query_place = iota((SEQ_LEN, SEQ_LEN), 0), iota((SEQ_LEN, SEQ_LEN), 1)
        for step in range(MICRO):
            normed_ref[step] = normed[spans[step]]
            query_ref[step] = query[spans[step]].T.astype(bf16)
            key_ref[step] = key[spans[step]].T.astype(bf16)
            value_ref[step] = value[spans[step]].T.astype(bf16)
            start = starts_ref[step]
            inside = (
                (key_place >= start)
                & (key_place < start + PIC)
                & (query_place >= start)
                & (query_place < start + PIC)
            )
            mask_ref[step] = jnp.where((key_place <= query_place) | inside, 0.0, -1e30)
        rel = (heads_ref[...].astype(f32) * narrow_ref[experts + 2 : experts + 3, :].astype(f32)).astype(bf16)
        table_ref[...] = dot_nn(dot_nn(rel, bucket_ref[...]).astype(bf16), hot_ref[...])

    span = pl.ds(pl.multiple_of(head * HEAD_DIM, HEAD_DIM), HEAD_DIM)
    table = jnp.broadcast_to(table_ref[pl.ds(head, 1), :], (8, 1024))
    low_row = iota((8, 1024), 0)
    for bit in (1, 2, 4):
        table = jnp.where((low_row & bit) != 0, pltpu.roll(table, bit, 1), table)
    for shift in (8, 16, 32, 64):
        table = jnp.concatenate([table, pltpu.roll(table, shift, 1)], axis=0)
    bias = jnp.concatenate([table[:, 384 - a * 128 : 896 - a * 128] for a in range(4)], axis=0)
    for step in range(MICRO):
        scores = dot_tn(key_ref[step, span, :], query_ref[step, span, :])
        scores = scores + bias + mask_ref[step]
        expo = jnp.exp(scores - jnp.max(scores, axis=0, keepdims=True))
        probs = (expo * (1.0 / jnp.sum(expo, axis=0, keepdims=True))).astype(bf16)
        probs_ref[step, 0] = probs
        attended_ref[step, span, :] = dot_nn(value_ref[step, span, :], probs).astype(bf16)

    @pl.when(head == HEADS - 1)
    def _():
        place = iota((experts, TOK_MB), 0)
        each = len(block_refs) // MICRO
        for step in range(MICRO):
            hidden = x_ref[spans[step], :].astype(f32) + dot_tn(attended_ref[step], out_w[0])
            hidden_ref[step] = hidden
            scale = lax.rsqrt(jnp.mean(hidden * hidden, axis=-1, keepdims=True) + epsilon)
            rows = (hidden * scale * narrow_ref[experts + 1 : experts + 2, :].astype(f32)).astype(bf16)
            router = dot_nt(narrow_ref[:experts, :], rows)
            chosen = [
                jnp.sum(jnp.where(ids_ref[k : k + 1, spans[step]] == place, router, 0.0), axis=0, keepdims=True)
                for k in range(TOP)
            ]
            gates_ref[step, 0:1, :] = 1.0 / (1.0 + jnp.exp(chosen[1] - chosen[0]))
            gates_ref[step, 1:2, :] = 1.0 / (1.0 + jnp.exp(chosen[0] - chosen[1]))
            blocks = block_refs[step * each : (step + 1) * each]
            half = blocks[0].shape[0] // (4 // each)
            for first in range(0, 4 * half, half):
                hots = [slot_hot(slots_ref[step, k : k + 1, :], first, half) for k in range(TOP)]
                value = dot_nn(jnp.where(hots[0] | hots[1], 1.0, 0.0).astype(bf16), rows).astype(bf16)
                low = first // 2
                if each == 1:
                    blocks[0][first : first + half, :] = value
                else:
                    blocks[0][low : low + half // 2, :] = value[: half // 2]
                    blocks[1][low : low + half // 2, :] = value[half // 2 :]


def matrix_specs():
    return [
        pl.BlockSpec((1, D, D), functools.partial(lambda i, h: (i, 0, 0), i), pipeline_mode=pl.Buffered(1))
        for i in range(4)
    ]


def attend(starts, tokens, matrices, narrow, constants, ids, slots, direct, experts, capacity):
    size = experts * capacity // (1 + direct)
    out_shapes = (
        [((MICRO, D, TOK_MB), bf16)] * 3
        + [((MICRO, HEADS, SEQ_LEN, SEQ_LEN), bf16), ((MICRO, D, TOK_MB), bf16), ((MICRO, TOK_MB, D), f32)]
        + [((MICRO, TOP, TOK_MB), f32), ((MICRO, TOK_MB, D), bf16)]
        + [((size, D), bf16)] * (MICRO * (1 + direct))
    )

    def whole(shape):
        return resident(shape, lambda h: (0,) * len(shape))

    out_specs = [
        pl.BlockSpec((MICRO, 1, SEQ_LEN, SEQ_LEN), lambda h: (0, h, 0, 0)) if len(s) == 4 else whole(s)
        for s, _ in out_shapes
    ]
    return pl.pallas_call(
        functools.partial(attend_kernel, experts=experts),
        grid=(HEADS,),
        in_specs=[pl.BlockSpec(memory_space=pltpu.SMEM), whole(tokens.shape)]
        + matrix_specs()
        + [whole(a.shape) for a in (narrow, *constants, ids, slots)],
        out_specs=out_specs,
        out_shape=[jax.ShapeDtypeStruct(*s) for s in out_shapes],
        scratch_shapes=[pltpu.VMEM((MICRO, SEQ_LEN, SEQ_LEN), f32), pltpu.VMEM((16, 1024), f32)],
        compiler_params=pltpu.CompilerParams(vmem_limit_bytes=58 * MIB),
        cost_estimate=lasting(42),
        name="attend",
    )(starts, tokens, *[matrices] * 4, narrow, *constants, ids, slots)


def collect(target, direct, passed, size):
    if passed is None:
        for index, ref in enumerate(direct):
            target[index * ref.shape[0] : (index + 1) * ref.shape[0], :] = ref[...]
        return
    for index, ref in enumerate(direct):
        low = 2 * index * size
        target[low : low + size, :] = ref[...]
        target[low + size : low + 2 * size, :] = passed[index * size : (index + 1) * size, :]


def received_specs(received, blocks, size):
    first = lambda *_: (0, 0)
    return [resident((size, D), first)] * blocks + [resident(r.shape, first) for r in received[blocks:]]


def expert_kernel(place_ref, *refs, blocks, passes, micro):
    accumulate = micro > 0
    rows_refs, cot_refs, refs = refs[:blocks], refs[blocks : 2 * blocks + passes], refs[2 * blocks + passes :]
    other_ref, router_ref, in_ref, out_ref = refs[:4]
    refs = refs[4:]
    if accumulate:
        prior, refs = refs[:5], refs[5:]
    grads, refs = refs[:5], refs[5:]
    result_refs, back_refs = refs[:blocks], refs[blocks : 2 * blocks]
    rows, picks, rows_t, gate_column, result, back, active, inner_grad = refs[2 * blocks :]
    step, me = pl.program_id(0), place_ref[0]
    total, tile = rows.shape[0], ROW_TILE
    senders, capacity = other_ref.shape
    experts = grads[4].shape[0]
    width = capacity if passes else total
    place = iota((experts, width), 0)

    @pl.when(step == 0)
    def _():
        collect(rows, rows_refs, None, width)
        collect(picks, cot_refs[:blocks], cot_refs[blocks] if passes else None, width)
        for sender in range(senders):
            here = slice(sender * width, (sender + 1) * width)
            logits = dot_nt(router_ref[:experts, :], rows[here, :])
            other = other_ref[sender : sender + 1, :].astype(jnp.int32)
            own_logit = jnp.sum(jnp.where(place == me, logits, 0.0), axis=0, keepdims=True)
            other_logit = jnp.sum(jnp.where(place == other, logits, 0.0), axis=0, keepdims=True)
            column = row_to_column(1.0 / (1.0 + jnp.exp(other_logit - own_logit)))
            gate_column[here, :] = column
            picks[here, :] = (picks[here, :].astype(f32) * column).astype(bf16)
        for low in range(0, total, tile):
            rows_t[:, low : low + tile] = rows[low : low + tile, :].astype(f32).T.astype(bf16)
        result[...] = jnp.zeros_like(result)
        back[...] = jnp.zeros_like(back)

    def one_tile(index):
        here = slice(index * tile, (index + 1) * tile)
        inner = dot_nn(rows[here, :], in_ref[0])
        square = inner * inner
        bend = jnp.tanh(inner * (0.7978845608028654 + 0.035677408136300125 * square))
        half = 0.5 * inner
        low = (half + half * bend).astype(bf16)
        active[here, :] = low
        result[here, :] += dot_nn(low, out_ref[0])
        slope = 0.5 + 0.5 * bend + half * (1.0 - bend * bend) * (0.7978845608028654 + 0.1070322244089004 * square)
        grad = (dot_nt(picks[here, :], out_ref[0]) * slope).astype(bf16)
        inner_grad[here, :] = grad
        back[here, :] += dot_nt(grad, in_ref[0])

    for index in range(total // tile):
        one_tile(index)

    def store(index, where, value):
        if accumulate:
            value = value + prior[index][where].astype(f32)
        grads[index][where] = value.astype(bf16)

    quarter = D // 4
    for index in range(4):
        first = pl.multiple_of((index ^ place_ref[1]) * quarter, quarter)
        store(index // 2, index % 2, dot_nn(rows_t[pl.ds(first, quarter), :], inner_grad[...]))
    outer = dot_tn(active[...], picks[...])

    @pl.when(step >= 2)
    def _():
        store(2, 0, outer)

    @pl.when(step < 2)
    def _():
        store(3, 0, outer)

    @pl.when(step == pl.num_programs(0) - 1)
    def _():
        router_sum = prior[4][...] if accumulate else jnp.zeros((experts, D), f32)
        for sender in range(senders):
            here = slice(sender * width, (sender + 1) * width)
            low = result[here, :].astype(bf16)
            score = jnp.sum(low.astype(f32) * picks[here, :].astype(f32), axis=-1, keepdims=True)
            choice = column_to_row((1.0 - gate_column[here, :]) * score)
            other = other_ref[sender : sender + 1, :].astype(jnp.int32)
            logit_grad = jnp.where(place == me, choice, 0.0) - jnp.where(place == other, choice, 0.0)
            logit_grad = logit_grad.astype(bf16)
            router_sum = router_sum + dot_nn(logit_grad, rows[here, :])
            total_back = back[here, :] + dot_tn(logit_grad, router_ref[:experts, :])
            index, first = (sender // 2, sender % 2 * width) if passes else (0, 0)
            back_refs[index][first : first + width, :] = total_back.astype(bf16)
            result_refs[index][first : first + width, :] = low
        grads[4][...] = router_sum


def run_expert(place, rows_blocks, cot_blocks, other, narrow, expert_in, expert_out, prior, micro, blocks, experts):
    passes = len(cot_blocks) - blocks
    size = rows_blocks[0].shape[0]
    total = blocks * size
    fixed = lambda i, place: (0, 0)
    chunk, quarter = FF // 4, D // 4
    at = lambda i, place: i ^ 2 ^ place[2]
    weights = [
        pl.BlockSpec((1, D, chunk), lambda i, place: (0, 0, at(i, place))),
        pl.BlockSpec((1, chunk, D), lambda i, place: (0, at(i, place), 0)),
    ]
    grad_specs = [
        pl.BlockSpec((2, quarter, chunk), lambda i, place: (0, 0, at(i, place))),
        pl.BlockSpec((2, quarter, chunk), lambda i, place: (0, 0, at(i, place))),
        pl.BlockSpec((1, chunk, D), lambda i, place: (jnp.maximum(i - 2, 0), 0, 0)),
        pl.BlockSpec((1, chunk, D), lambda i, place: (jnp.minimum(i, 1), 0, 0)),
        resident((experts, D), fixed),
    ]
    grad_shapes = [((2, quarter, FF), bf16)] * 2 + [((2, chunk, D), bf16)] * 2 + [((experts, D), f32)]
    taken = received_specs(rows_blocks, blocks, size)
    taken += received_specs(cot_blocks, blocks, size // (1 + passes))
    out = pl.pallas_call(
        functools.partial(expert_kernel, blocks=blocks, passes=passes, micro=micro),
        grid_spec=pltpu.PrefetchScalarGridSpec(
            num_scalar_prefetch=1,
            grid=(4,),
            in_specs=taken
            + [resident(other.shape, fixed), resident(narrow.shape, fixed)]
            + weights
            + (grad_specs if prior else []),
            out_specs=grad_specs + [resident((size, D), fixed)] * (2 * blocks),
            scratch_shapes=[
                pltpu.VMEM((total, D), bf16),
                pltpu.VMEM((total, D), bf16),
                pltpu.VMEM((D, total), bf16),
                pltpu.VMEM((total, 1), f32),
                pltpu.VMEM((total, D), f32),
                pltpu.VMEM((total, D), f32),
                pltpu.VMEM((total, chunk), bf16),
                pltpu.VMEM((total, chunk), bf16),
            ],
        ),
        out_shape=[jax.ShapeDtypeStruct(*s) for s in grad_shapes]
        + [jax.ShapeDtypeStruct((size, D), bf16)] * (2 * blocks),
        compiler_params=pltpu.CompilerParams(vmem_limit_bytes=62 * MIB),
        cost_estimate=lasting(62),
        name="expert",
    )(place, *rows_blocks, *cot_blocks, other, narrow, expert_in, expert_out, *(prior or ()))
    return out[:5], out[5:]


def trade(value, groups, mask):
    return lax.ppermute(value, "group", swap(groups, mask))


def add_low(left, right):
    return (left.astype(f32) + right.astype(f32)).astype(bf16)


def second_half(half, groups, mask):
    return add_low(half[0], trade(half[1], groups, mask))


def spread_kernel(place_ref, own_ref, beside_ref, far_ref, out_ref, *, code):
    index = pl.program_id(0) ^ place_ref[code]

    @pl.when(index == 0)
    def _():
        out_ref[...] = own_ref[...].astype(f32)

    @pl.when(index == 1)
    def _():
        out_ref[...] = beside_ref[...].astype(f32)

    @pl.when(index > 1)
    def _():
        out_ref[...] = far_ref[...].astype(f32)


def spread_pieces(place, pieces, code):
    shape = pieces[0].shape[1:]
    block = (1, *shape)
    return pl.pallas_call(
        functools.partial(spread_kernel, code=code),
        grid_spec=pltpu.PrefetchScalarGridSpec(
            num_scalar_prefetch=1,
            grid=(4,),
            in_specs=[pl.BlockSpec(block, lambda i, place: (0, 0, 0))] * 2
            + [pl.BlockSpec(block, lambda i, place: ((i ^ place[code]) & 1, 0, 0))],
            out_specs=pl.BlockSpec(block, lambda i, place: (i, 0, 0)),
        ),
        out_shape=jax.ShapeDtypeStruct((4, *shape), f32),
        compiler_params=pltpu.CompilerParams(vmem_limit_bytes=32 * MIB),
        cost_estimate=lasting(6),
        name="spread",
    )(place, *pieces)


def back_kernel(*refs, blocks, passes, experts, devices, final):
    me_ref, refs = refs[0], refs[1:]
    take = blocks + passes
    back_refs, refs = refs[:take], refs[take:]
    (x_ref, cot_ref, query_w, key_w, value_w, out_w, narrow_ref, hot_ref, bucket_ref, heads_ref, slots_ref) = refs[:11]
    (query_ref, key_ref, value_ref, probs_ref, attended_ref, hidden_ref, normed_ref) = refs[11:18]
    refs = refs[18:]
    if final:
        prior, router_grad, refs = refs[: 1 + passes], refs[1 + passes], refs[2 + passes :]
    token_ref, dense_refs, refs = refs[0], refs[1 : 2 + passes], refs[2 + passes :]
    gathered, hidden_grad, out_grad, query_grad, key_grad, value_grad, whole, lines, diagonals = refs
    head = pl.program_id(0)
    total = gathered.shape[0]

    def dense(first, value):
        columns = slice(first, first + value.shape[1])
        if not passes:
            if final:
                value = value + prior[0][:, columns].astype(f32)
            dense_refs[0][:, columns] = value.astype(bf16)
            return
        whole[:, : value.shape[1]] = value
        rows = D // devices
        for k in range(devices):
            start = pl.multiple_of((me_ref[0] ^ k) * rows, 32)
            piece = whole[pl.ds(start, rows), : value.shape[1]]
            here = slice(k // 2 * rows, (k // 2 + 1) * rows)
            if final:
                piece = piece + prior[k % 2][here, columns].astype(f32)
            dense_refs[k % 2][here, columns] = piece.astype(bf16)

    @pl.when(head == 0)
    def _():
        lines[...] = jnp.zeros_like(lines)
        diagonals[...] = jnp.zeros_like(diagonals)
        cot = cot_ref[...].astype(f32)
        collect(gathered, back_refs[:blocks], back_refs[blocks] if passes else None, back_refs[0].shape[0])
        columns = [row_to_column(slots_ref[k : k + 1, :].astype(f32)).astype(jnp.int32) for k in range(TOP)]
        rows_grad = jnp.zeros((TOK_MB, D), f32)
        for low in range(0, total, 512):
            place = iota((TOK_MB, 512), 1) + low
            pick = jnp.where((place == columns[0]) | (place == columns[1]), 1.0, 0.0).astype(bf16)
            rows_grad = rows_grad + dot_nn(pick, gathered[low : low + 512, :])
        hidden = hidden_ref[...]
        scale = lax.rsqrt(jnp.mean(hidden * hidden, axis=-1, keepdims=True) + epsilon)
        normal = hidden * scale
        lines[experts + 1 : experts + 2, :] = jnp.sum(rows_grad * normal, axis=0, keepdims=True)
        scaled = rows_grad * narrow_ref[experts + 1 : experts + 2, :].astype(f32)
        total_grad = cot + scale * (scaled - normal * jnp.mean(scaled * normal, axis=-1, keepdims=True))
        hidden_grad[...] = total_grad
        branch = total_grad.astype(bf16)
        dense(3 * D, dot_nn(attended_ref[...], branch))
        out_grad[...] = dot_nt(out_w[0], branch).astype(bf16)

    span = pl.ds(pl.multiple_of(head * HEAD_DIM, HEAD_DIM), HEAD_DIM)
    low = probs_ref[0]
    grad_here = out_grad[span, :]
    probs = low.astype(f32)
    value_grad[span, :] = dot_nt(grad_here, low).astype(bf16)
    prob_grad = dot_tn(value_ref[span, :], grad_here)
    center = jnp.sum(probs * prob_grad, axis=0, keepdims=True)
    score_grad = (probs * (prob_grad - center)).astype(bf16)
    query_grad[span, :] = (dot_nn(key_ref[span, :], score_grad) * HEAD_DIM**-0.5).astype(bf16)
    key_grad[span, :] = dot_nt(query_ref[span, :], score_grad).astype(bf16)
    wide = score_grad.astype(f32)
    chunks = []
    for place in range(-3, 4):
        parts = [
            wide[a * 128 : a * 128 + 128, (a + place) * 128 : (a + place) * 128 + 128]
            for a in range(4)
            if 0 <= a + place < 4
        ]
        chunks.append(sum(parts[1:], parts[0]))
    folded = jnp.concatenate([*chunks, jnp.zeros((128, 128), f32)], axis=1)
    for half in (64, 32, 16, 8):
        folded = folded[:half] + pltpu.roll(folded[half:], 1024 - half, 1)
    low_row = iota((8, 1024), 0)
    for bit in (4, 2, 1):
        folded = jnp.where((low_row & bit) != 0, pltpu.roll(folded, 1024 - bit, 1), folded)
    diagonals[pl.ds(head, 1), :] = jnp.sum(folded, axis=0, keepdims=True)

    @pl.when(head == HEADS - 1)
    def _():
        normed_t = normed_ref[...].astype(f32).T.astype(bf16)
        grads = (query_grad[...], key_grad[...], value_grad[...])
        in_grad = jnp.zeros((D, TOK_MB), f32)
        for i, (grad, weight) in enumerate(zip(grads, (query_w, key_w, value_w))):
            dense(i * D, dot_nt(normed_t, grad))
            in_grad = in_grad + dot_nn(weight[0], grad)
        in_grad = in_grad.T
        x = x_ref[...].astype(f32)
        scale = lax.rsqrt(jnp.mean(x * x, axis=-1, keepdims=True) + epsilon)
        normal = x * scale
        lines[experts : experts + 1, :] = jnp.sum(in_grad * normal, axis=0, keepdims=True)
        scaled = in_grad * narrow_ref[experts : experts + 1, :].astype(f32)
        grad = hidden_grad[...] + scale * (scaled - normal * jnp.mean(scaled * normal, axis=-1, keepdims=True))
        token_ref[...] = grad.astype(bf16)
        if final:
            lines[:experts, :] = router_grad[...]
        by_bucket = sum_dot(diagonals[...], hot_ref[...], dot_nt)
        by_place = sum_dot(by_bucket, bucket_ref[...], dot_nt)
        lines[experts + 2 : experts + 3, :] = jnp.sum(by_place * heads_ref[...].astype(f32), axis=0, keepdims=True)
        dense(4 * D, lines[...].T)


def sum_dot(values, hot, dot):
    high = values.astype(bf16)
    return dot(high, hot) + dot((values - high.astype(f32)).astype(bf16), hot)


def backward(me, back_blocks, tokens, cotangent, matrices, narrow, constants, slots, saved, prior, step, blocks, experts, devices, slot_count):
    passes = len(back_blocks) - blocks
    size = slot_count // blocks // (1 + passes)
    fixed = lambda h: (0, 0)
    block = lambda h: (step, 0)
    head_block = pl.BlockSpec((None, 1, SEQ_LEN, SEQ_LEN), lambda h: (step, h, 0, 0))
    wide = 4 * D + 128
    dense_shapes = [(D // (1 + passes), wide)] * (1 + passes)
    dense_specs = [resident(s, fixed) for s in dense_shapes]
    return pl.pallas_call(
        functools.partial(
            back_kernel, blocks=blocks, passes=passes, experts=experts, devices=devices, final=prior is not None
        ),
        grid=(HEADS,),
        in_specs=[pl.BlockSpec(memory_space=pltpu.SMEM)]
        + received_specs(back_blocks, blocks, size)
        + [resident((TOK_MB, D), block)] * 2
        + matrix_specs()
        + [resident(narrow.shape, fixed)]
        + [resident(c.shape, fixed) for c in constants]
        + [resident((TOP, TOK_MB), fixed)]
        + [head_block if s.ndim == 4 else resident((None, *s.shape[1:]), lambda h: (step, 0, 0)) for s in saved]
        + (dense_specs + [resident((experts, D), fixed)] if prior else []),
        out_specs=[resident((TOK_MB, D), fixed)] + dense_specs,
        out_shape=[jax.ShapeDtypeStruct((TOK_MB, D), bf16)] + [jax.ShapeDtypeStruct(s, bf16) for s in dense_shapes],
        scratch_shapes=[
            pltpu.VMEM((slot_count, D), bf16),
            pltpu.VMEM((TOK_MB, D), f32),
            pltpu.VMEM((D, TOK_MB), bf16),
            pltpu.VMEM((D, TOK_MB), bf16),
            pltpu.VMEM((D, TOK_MB), bf16),
            pltpu.VMEM((D, TOK_MB), bf16),
            pltpu.VMEM((D, D), f32),
            pltpu.VMEM((128, D), f32),
            pltpu.VMEM((16, 1024), f32),
        ],
        compiler_params=pltpu.CompilerParams(vmem_limit_bytes=58 * MIB),
        cost_estimate=lasting(34),
        name="backward",
    )(me, *back_blocks, tokens, cotangent, *[matrices] * 4, narrow, *constants, slots, *saved, *(prior or ()))


def combine_kernel(*refs, blocks, passes):
    result_refs = refs[: blocks + passes]
    hidden_ref, slots_ref, gates_ref, mixed_ref, gathered = refs[blocks + passes :]
    size = result_refs[0].shape[0]
    collect(gathered, result_refs[:blocks], result_refs[blocks] if passes else None, size)
    slots = [row_to_column(slots_ref[k : k + 1, :].astype(f32)).astype(jnp.int32) for k in range(TOP)]
    gates = [row_to_column(gates_ref[k : k + 1, :]) for k in range(TOP)]
    output = hidden_ref[...]
    for k in range(TOP):
        picked = jnp.zeros((TOK_MB, D), f32)
        for low in range(0, gathered.shape[0], 512):
            pick = jnp.where(iota((TOK_MB, 512), 1) + low == slots[k], 1.0, 0.0).astype(bf16)
            picked = picked + dot_nn(pick, gathered[low : low + 512, :])
        output = output + gates[k] * picked
    mixed_ref[...] = output.astype(bf16)


def combine(received, hidden, slots, gates, step, blocks, slot_count):
    passes = len(received) - blocks
    size = slot_count // blocks // (1 + passes)
    fixed = lambda i: (0, 0)
    return pl.pallas_call(
        functools.partial(combine_kernel, blocks=blocks, passes=passes),
        grid=(1,),
        in_specs=received_specs(received, blocks, size)
        + [resident((None, *a.shape[1:]), lambda i: (step, 0, 0)) for a in (hidden, slots, gates)],
        out_specs=resident((TOK_MB, D), fixed),
        out_shape=jax.ShapeDtypeStruct((TOK_MB, D), bf16),
        scratch_shapes=[pltpu.VMEM((slot_count, D), bf16)],
        compiler_params=pltpu.CompilerParams(vmem_limit_bytes=32 * MIB),
        cost_estimate=lasting(3),
        name="combine",
    )(*received, hidden, slots, gates)


def tie(values, *after):
    count = len(values)
    return list(lax.optimization_barrier((*values, *after)))[:count]


def send(blocks, devices):
    if len(blocks) == 1:
        whole = blocks[0]
        moved = whole.reshape(devices, -1, D)
        moved = lax.all_to_all(moved, "expert", split_axis=0, concat_axis=0, tiled=True)
        return [moved.reshape(whole.shape)]
    return [blocks[0]] + [
        lax.ppermute(blocks[j], "expert", swap(devices, 2 * j)) for j in range(1, len(blocks))
    ]


def pair_up(near, cross, devices):
    got = lax.ppermute(cross, "expert", swap(devices, 1))
    size = 2 * near.shape[0] // devices
    return [jnp.concatenate([a[low : low + size] for a in (near, got)]) for low in range(0, near.shape[0], size)]


def pass_on(blocks, devices):
    if len(blocks) == 1:
        return blocks
    half = blocks[0].shape[0] // 2
    second = jnp.concatenate([b[half:] for b in blocks], axis=0)
    return [*blocks, lax.ppermute(second, "expert", swap(devices, 1))]


def sum_cores(pieces, devices):
    near, cross = pieces
    return near.astype(f32) + lax.ppermute(cross, "expert", swap(devices, 1)).astype(f32)


def sum_chips(own, low, devices):
    chips = devices // 2
    rows = low.shape[0] // chips
    for j in range(1, chips):
        own = own + lax.ppermute(low[j * rows : (j + 1) * rows], "expert", swap(devices, 2 * j)).astype(f32)
    return own


def reduce_group(total, groups, *after):
    parts, masks = [total[:, : 2 * D], total[:, 2 * D :]], [1, 2]
    for turn in range(2):
        low = [part.astype(bf16) for part in parts]
        if turn:
            low = tie(low, *after)
        parts = [
            here.astype(f32) + lax.ppermute(here, "group", swap(groups, mask)).astype(f32)
            for here, mask in zip(low, masks)
        ]
        masks = masks[::-1]
    return parts


def shards(
    tokens, cotangent, norm_attn, w_query, w_key, w_value, w_out, rel_bias, norm_expert, w_router,
    expert_in, expert_out, expert_ids, span_starts,
):
    experts = w_router.shape[1]
    capacity = 3 * TOK_MB * TOP // (2 * experts)
    groups, devices = lax.axis_size("group"), lax.axis_size("expert")
    direct = devices <= DIRECT_MAX
    blocks = devices // 2 if direct else 1
    shard, share = w_query.shape[0], rel_bias.shape[0]
    me = lax.axis_index("expert").reshape(1).astype(jnp.int32)
    order = me if direct else jnp.zeros_like(me)
    ids = expert_ids.T
    group = lax.axis_index("group").reshape(1).astype(jnp.int32)
    place = jnp.concatenate([me, group % 2 * 2 + group // 2, group])

    padded = jnp.pad(rel_bias, (0, shard - share))
    narrow = jnp.concatenate([w_router.T, norm_attn[None], norm_expert[None], padded[None]], axis=0)
    slots, cots = route(order, ids, cotangent, blocks, experts, capacity)
    matrices, narrow, all_ids, cots[0] = gather_weights(
        (w_query, w_key, w_value, w_out), narrow, ids, cots[0], groups, devices
    )
    bucket, heads = bias_places(devices)
    constants = (bucket_hot().astype(bf16), bucket.astype(bf16), heads.astype(bf16))
    slot_count = experts * capacity
    cots[1] = send(tie(cots[1], *cots[0][1:]), devices)
    other = partners(me, all_ids, devices, capacity, direct)
    if not direct:
        other = other.reshape(MICRO, 1, slot_count)
    (narrow,) = tie([narrow], *cots[0][1:], other)
    *saved, = attend(span_starts, tokens, matrices, narrow, constants, ids, slots, direct, experts, capacity)
    saved, sent = saved[:8], saved[8:]
    sent = [sent[step * (1 + direct) : (step + 1) * (1 + direct)] for step in range(MICRO)]
    cots[1] = tie(cots[1], saved[0])
    if direct:
        sent = [pair_up(*tie(s, *cots[1][1:]), devices) for s in sent]
    sent[0] = send(tie(sent[0], *cots[1][1:]), devices)
    cots = [pass_on(tie(c, saved[0]), devices) for c in cots]
    sent[1] = send(tie(sent[1], *sent[0][1:]), devices)

    grads, first = run_expert(
        place, sent[0], cots[0], other[0], narrow, expert_in, expert_out, None, 0, blocks, experts
    )
    sent[1] = tie(sent[1], first[0])
    results, backs = [first[:blocks]], [send(tie(first[blocks:], *sent[1]), devices)]
    grads, last = run_expert(
        place, sent[1], cots[1], other[1], narrow, expert_in, expert_out, grads, 1, blocks, experts
    )
    results.append(last[:blocks])
    backs.append(last[blocks:])
    *flat, router_grad = tie(grads, *backs[0][1:])
    away = [trade(flat[1], groups, 1), trade(flat[3], groups, 2)]
    backs[0] = pass_on(tie(backs[0], last[0]), devices)
    backs[1] = send(tie(backs[1], *backs[0]), devices)

    def run_back(step, prior):
        query, key, value, probs, attended, hidden, _, normed = saved
        return backward(
            order, backs[step], tokens, cotangent, matrices, narrow, constants, slots[step],
            (query, key, value, probs, attended, hidden, normed), prior, step, blocks, experts, devices, slot_count,
        )

    token_grads = [None, None]
    token_grads[0], *dense = run_back(0, None)
    backs[1] = pass_on(tie(backs[1], token_grads[0]), devices)
    away = tie(away, *backs[1])
    halves = [add_low(flat[0], away[0]), add_low(flat[2], away[1])]
    owns = [second_half(halves[0], groups, 2), second_half(halves[1], groups, 1)]
    if direct:
        results[0] = send(tie(results[0], *backs[1]), devices)
    else:
        results = [send(r, devices) for r in results]
    backs[1] = tie(backs[1], *halves)
    token_grads[1], *dense = run_back(1, (*dense, router_grad))
    owns = tie(owns, token_grads[1], *results[0])
    if direct:
        results[0] = pass_on(tie(results[0], token_grads[1]), devices)
    if direct:
        dense = tie(dense, *results[0][1:-1], *owns)
        total = sum_cores(dense, devices)
        low = total.astype(bf16)
        owns = tie(owns, low)
    besides = [trade(owns[0], groups, 2), trade(owns[1], groups, 1)]
    fars = [jnp.stack(pair) for pair in zip(owns, besides)]
    if direct:
        total = sum_chips(total[:shard], low, devices)
        results[1] = send(tie(results[1], total), devices)
        (total,) = tie([total], results[1][1])
        results[1] = pass_on(results[1], devices)
    else:
        total = lax.psum_scatter(dense[0], "expert", scatter_dimension=0, tiled=True).astype(f32)
    fars = [trade(fars[0], groups, 1), trade(fars[1], groups, 2)]
    inward, outward = [(own[None], beside[None], far) for own, beside, far in zip(owns, besides, fars)]
    mixed = [
        combine(results[step], saved[5], slots, saved[6], step, blocks, slot_count)
        for step in range(MICRO)
    ]
    (total,) = tie([total], mixed[0])
    grad_in = spread_pieces(place, inward, 1).reshape(expert_in.shape)
    grad_out = spread_pieces(place, outward, 2).reshape(expert_out.shape)
    total = reduce_group(total, groups, grad_in, grad_out)
    first, second = total
    thin = second[:, 2 * D :]
    return (
        jnp.concatenate(mixed, axis=0),
        jnp.concatenate(token_grads, axis=0),
        thin[:, experts],
        first[:, :D],
        first[:, D:],
        second[:, :D],
        second[:, D : 2 * D],
        thin[:share, experts + 2],
        thin[:, experts + 1],
        thin[:, :experts],
        grad_in,
        grad_out,
    )


def solution(mesh):
    rows, split = P(("group", "expert"), None), P("expert", None)
    stacked = P("expert", None, None)
    return jax.shard_map(
        shards,
        mesh=mesh,
        in_specs=(
            rows, rows, P("expert"), split, split, split, split, P("expert"), P("expert"), split,
            stacked, stacked, rows, P(("group", "expert")),
        ),
        out_specs=(
            rows, rows, P("expert"), split, split, split, split, P("expert"), P("expert"), split, stacked, stacked,
        ),
        check_vma=False,
    )
```

```python
import functools

import jax
import jax.numpy as jnp
import numpy as np
from jax import lax
from jax.experimental import pallas as pl
from jax.experimental.pallas import tpu as pltpu
from jax.sharding import PartitionSpec as P

D = 768
HEADS = 12
HEAD_DIM = 64
FF = 3072
TOP = 2
BUCKETS = 32
SEQ_LEN = 512
PIC = 256
MICRO = 2
TOK_MB = 512
ROW_TILE = 256
DIRECT_MAX = 8
COST_BYTES = 3600000

epsilon = 1e-06
bucket_edges = (1, 2, 3, 4, 5, 6, 7, 8, 12, 16, 23, 32, 45, 64, 91)
f32 = jnp.float32
bf16 = jnp.bfloat16
MIB = 1 << 20


def dot_nn(left, right):
    return lax.dot_general(left, right, (((1,), (0,)), ((), ())), preferred_element_type=f32)


def dot_nt(left, right):
    return lax.dot_general(left, right, (((1,), (1,)), ((), ())), preferred_element_type=f32)


def dot_tn(left, right):
    return lax.dot_general(left, right, (((0,), (0,)), ((), ())), preferred_element_type=f32)


def iota(shape, dim):
    return lax.broadcasted_iota(jnp.int32, shape, dim)


def diagonal_offsets():
    place = np.arange(1024)
    return np.where(place < 896, 384 - place, 1408 - place)


def bucket_hot():
    offset = diagonal_offsets()
    magnitude = sum((np.abs(offset) >= edge).astype(np.int32) for edge in bucket_edges)
    bucket = magnitude + 16 * (offset > 0)
    hot = bucket[None, :] == np.arange(BUCKETS)[:, None]
    return hot & (np.abs(offset) < SEQ_LEN)[None, :]


def lasting(microseconds):
    return pl.CostEstimate(flops=0, bytes_accessed=int(microseconds * COST_BYTES), transcendentals=0)


def resident(shape, index):
    return pl.BlockSpec(shape, index, pipeline_mode=pl.Buffered(1))


def split_rows(values):
    high = values.astype(bf16).astype(f32)
    row = iota((8, values.shape[1]), 0)
    return jnp.where(row == 0, high, jnp.where(row == 1, values - high, 0.0)).astype(bf16)


def row_to_column(row):
    size = row.shape[1]
    step = 128 if size % 128 == 0 else size
    eye = iota((step, step), 0) == iota((step, step), 1)
    columns = [
        jnp.sum(jnp.where(eye, row[:, i : i + step], 0.0), axis=1, keepdims=True)
        for i in range(0, size, step)
    ]
    return columns[0] if len(columns) == 1 else jnp.concatenate(columns, axis=0)


def column_to_row(column):
    size = column.shape[0]
    step = 128 if size % 128 == 0 else size
    eye = iota((step, step), 0) == iota((step, step), 1)
    rows = [
        jnp.sum(jnp.where(eye, column[i : i + step], 0.0), axis=0, keepdims=True)
        for i in range(0, size, step)
    ]
    return rows[0] if len(rows) == 1 else jnp.concatenate(rows, axis=1)


def slot_hot(slot_row, first, size):
    return iota((size, TOK_MB), 0) + first == slot_row


def route_kernel(me_ref, ids_ref, cot_ref, slots_ref, *block_refs, experts, capacity):
    place = iota((experts, TOK_MB), 0)
    earlier = earlier_places()
    for step in range(MICRO):
        here = slice(step * TOK_MB, (step + 1) * TOK_MB)
        hots = [ids_ref[k : k + 1, here] == place for k in range(TOP)]
        both = jnp.where(hots[0] | hots[1], 1.0, 0.0).astype(bf16)
        at = dot_nn(both, earlier) + ((place ^ me_ref[0]) * capacity).astype(f32)
        slots = [jnp.sum(jnp.where(hot, at, 0.0), axis=0, keepdims=True).astype(jnp.int32) for hot in hots]
        for k in range(TOP):
            slots_ref[step, k : k + 1, :] = slots[k]
        blocks = block_refs[step * len(block_refs) // MICRO : (step + 1) * len(block_refs) // MICRO]
        size = blocks[0].shape[0]
        for first in range(0, experts * capacity, 384):
            hot = slot_hot(slots[0], first, 384) | slot_hot(slots[1], first, 384)
            value = dot_nn(jnp.where(hot, 1.0, 0.0).astype(bf16), cot_ref[here, :]).astype(bf16)
            blocks[first // size][first % size : first % size + 384, :] = value


def earlier_places():
    return jnp.where(iota((TOK_MB, TOK_MB), 0) < iota((TOK_MB, TOK_MB), 1), 1.0, 0.0).astype(bf16)


def route(me, ids, cotangent, blocks, experts, capacity):
    size = experts * capacity // blocks
    slots, *out = pl.pallas_call(
        functools.partial(route_kernel, experts=experts, capacity=capacity),
        in_specs=[pl.BlockSpec(memory_space=pltpu.SMEM)] + [pl.BlockSpec(memory_space=pltpu.VMEM)] * 2,
        out_shape=[jax.ShapeDtypeStruct((MICRO, TOP, TOK_MB), jnp.int32)]
        + [jax.ShapeDtypeStruct((size, D), bf16)] * (MICRO * blocks),
        compiler_params=pltpu.CompilerParams(vmem_limit_bytes=32 * MIB),
        cost_estimate=lasting(4),
        name="route",
    )(me, ids, cotangent)
    return slots, [out[step * blocks : (step + 1) * blocks] for step in range(MICRO)]


def partner_kernel(me_ref, ids_ref, other_ref, *, xor):
    devices, capacity = other_ref.shape[1:]
    earlier = earlier_places()
    mine = me_ref[0].astype(f32)
    for step in range(MICRO):
        first, second = ids_ref[step], ids_ref[MICRO + step]
        hot = (first == mine) | (second == mine)
        order = dot_nn(jnp.where(hot, 1.0, 0.0).astype(bf16), earlier).astype(jnp.int32)
        order = jnp.where(hot, order, -1)
        partner = (first + second - mine).astype(bf16)
        for sender in range(devices):
            pick = jnp.where(iota((capacity, TOK_MB), 0) == order[sender : sender + 1, :], 1.0, 0.0).astype(bf16)
            found = dot_nt(partner, pick)[sender : sender + 1, :]
            row = sender ^ me_ref[0] if xor else sender
            other_ref[step, pl.ds(row, 1), :] = found


def partners(me, ids, devices, capacity, xor):
    return pl.pallas_call(
        functools.partial(partner_kernel, xor=xor),
        in_specs=[pl.BlockSpec(memory_space=pltpu.SMEM)] + [pl.BlockSpec(memory_space=pltpu.VMEM)],
        out_shape=jax.ShapeDtypeStruct((MICRO, devices, capacity), f32),
        compiler_params=pltpu.CompilerParams(vmem_limit_bytes=32 * MIB),
        cost_estimate=lasting(1.3),
        name="partners",
    )(me, ids)


def unpack_kernel(place_ref, *refs, groups, chips, lines):
    own, (passed, *smalls, out_ref, narrow_ref, ids_ref) = refs[:groups], refs[groups:]
    rows = own[0].shape[0] // chips
    me = place_ref[1]
    for k in range(groups):
        for j in range(chips):
            low = (k * chips + j) * rows
            values = own[k][j * rows : (j + 1) * rows, :], passed[low : low + rows, :]
            for core in range(2):
                here = pl.ds(pl.multiple_of((me ^ (2 * j + core)) * rows, rows), rows)
                out_ref[place_ref[0] ^ k, here, :] = values[core]
    gathered = jnp.zeros((16, D), f32)
    lane = iota((16, D), 1)
    for k in range(2 * chips):
        block = smalls[k % 2][k // 2 * 16 : k // 2 * 16 + 16, :].astype(f32)
        device = me ^ k
        gathered = gathered + pltpu.roll(jnp.where(lane < rows, block, 0.0), device * rows, 1)
        for pick in range(TOP * MICRO):
            ids_ref[pick, pl.ds(device, 1), :] = block[lines + pick : lines + pick + 1, :TOK_MB]
    narrow_ref[...] = gathered.astype(bf16)


def gather_weights(matrices, narrow, ids, blocks, groups, devices):
    lines, shard = narrow.shape
    if devices > DIRECT_MAX:
        whole = jnp.stack([lax.all_gather(w, "expert", axis=0, tiled=True) for w in matrices])
        flat = jnp.concatenate([narrow.reshape(-1), ids.astype(bf16).reshape(-1)])
        flat = lax.all_gather(flat, "expert", axis=0)
        narrow = flat[:, : lines * shard].reshape(devices, lines, shard).transpose(1, 0, 2).reshape(lines, D)
        ids = flat[:, lines * shard :].astype(f32).reshape(devices, TOP * MICRO, TOK_MB).transpose(1, 0, 2)
        return whole, narrow, ids, send(blocks, devices)
    chips = devices // 2
    group, me = lax.axis_index("group"), lax.axis_index("expert")
    mine = matrices[0]
    for index in range(1, groups):
        mine = jnp.where(group == index, matrices[index], mine)
    small = jnp.concatenate(
        [
            jnp.pad(narrow, ((0, 0), (0, D - shard))),
            jnp.pad(ids.astype(bf16).reshape(TOP * MICRO, TOK_MB), ((0, 0), (0, D - TOK_MB))),
            jnp.zeros((16 - lines - TOP * MICRO, D), bf16),
        ],
        axis=0,
    )
    mine = jnp.concatenate([mine, small], axis=0)
    mine = [mine] + [lax.ppermute(mine, "expert", swap(devices, 2 * j)) for j in range(1, chips)]
    small = jnp.concatenate([m[shard:] for m in mine], axis=0)
    mine = jnp.concatenate([m[:shard] for m in mine], axis=0)
    blocks = send(tie(blocks, mine), devices)
    near = lax.ppermute(mine, "group", swap(groups, 1))
    far = lax.ppermute(mine, "group", swap(groups, 2))
    near, far = tie([near, far], blocks[chips // 2])
    half = mine.shape[0] // 2
    low = lax.ppermute(far[:half], "group", swap(groups, 1))
    high = lax.ppermute(near[half:], "group", swap(groups, 2))
    own = [mine, near, far, jnp.concatenate([low, high], axis=0)]
    (passed,) = tie([jnp.concatenate(own, axis=0)], *blocks[1:])
    passed = lax.ppermute(passed, "expert", swap(devices, 1))
    passed_small = lax.ppermute(small, "expert", swap(devices, 1))
    place = jnp.stack([group, me]).astype(jnp.int32)
    whole, narrow, ids = pl.pallas_call(
        functools.partial(unpack_kernel, groups=groups, chips=chips, lines=lines),
        in_specs=[pl.BlockSpec(memory_space=pltpu.SMEM)] + [pl.BlockSpec(memory_space=pltpu.VMEM)] * (groups + 3),
        out_shape=[
            jax.ShapeDtypeStruct((groups, D, D), bf16),
            jax.ShapeDtypeStruct((16, D), bf16),
            jax.ShapeDtypeStruct((TOP * MICRO, devices, TOK_MB), f32),
        ],
        compiler_params=pltpu.CompilerParams(vmem_limit_bytes=32 * MIB),
        cost_estimate=lasting(3),
        name="unpack",
    )(place, *own, passed, small, passed_small)
    return whole, narrow, ids, blocks


def swap(devices, mask):
    return [(i, i ^ mask) for i in range(devices)]


def bias_places(devices):
    place = np.arange(D)
    wide, share = D // devices, HEADS * BUCKETS // devices
    flat = place // wide * share + place % wide
    used = place % wide < share
    bucket = (flat[:, None] % BUCKETS == np.arange(BUCKETS)[None, :]) & used[:, None]
    head = (flat[None, :] // BUCKETS == np.arange(16)[:, None]) & used[None, :]
    return bucket.astype(np.float32), head.astype(np.float32)


def attend_kernel(
    starts_ref, x_ref, query_w, key_w, value_w, out_w, narrow_ref, hot_ref, bucket_ref, heads_ref, ids_ref, slots_ref,
    query_ref, key_ref, value_ref, probs_ref, attended_ref, hidden_ref, gates_ref, normed_ref,
    *refs, experts,
):
    block_refs, (mask_ref, table_ref) = refs[:-2], refs[-2:]
    head = pl.program_id(0)
    spans = [slice(step * TOK_MB, (step + 1) * TOK_MB) for step in range(MICRO)]

    @pl.when(head == 0)
    def _():
        x = x_ref[...].astype(f32)
        scale = lax.rsqrt(jnp.mean(x * x, axis=-1, keepdims=True) + epsilon)
        normed = (x * scale * narrow_ref[experts : experts + 1, :].astype(f32)).astype(bf16)
        query = dot_nn(normed, query_w[0]).astype(bf16).astype(f32) * HEAD_DIM**-0.5
        key, value = dot_nn(normed, key_w[0]), dot_nn(normed, value_w[0])
        key_place, query_place = iota((SEQ_LEN, SEQ_LEN), 0), iota((SEQ_LEN, SEQ_LEN), 1)
        for step in range(MICRO):
            normed_ref[step] = normed[spans[step]]
            query_ref[step] = query[spans[step]].T.astype(bf16)
            key_ref[step] = key[spans[step]].T.astype(bf16)
            value_ref[step] = value[spans[step]].T.astype(bf16)
            start = starts_ref[step]
            inside = (
                (key_place >= start)
                & (key_place < start + PIC)
                & (query_place >= start)
                & (query_place < start + PIC)
            )
            mask_ref[step] = jnp.where((key_place <= query_place) | inside, 0.0, -1e30)
        rel = (heads_ref[...].astype(f32) * narrow_ref[experts + 2 : experts + 3, :].astype(f32)).astype(bf16)
        table_ref[...] = dot_nn(dot_nn(rel, bucket_ref[...]).astype(bf16), hot_ref[...])

    span = pl.ds(pl.multiple_of(head * HEAD_DIM, HEAD_DIM), HEAD_DIM)
    table = jnp.broadcast_to(table_ref[pl.ds(head, 1), :], (8, 1024))
    low_row = iota((8, 1024), 0)
    for bit in (1, 2, 4):
        table = jnp.where((low_row & bit) != 0, pltpu.roll(table, bit, 1), table)
    for shift in (8, 16, 32, 64):
        table = jnp.concatenate([table, pltpu.roll(table, shift, 1)], axis=0)
    bias = jnp.concatenate([table[:, 384 - a * 128 : 896 - a * 128] for a in range(4)], axis=0)
    for step in range(MICRO):
        scores = dot_tn(key_ref[step, span, :], query_ref[step, span, :])
        scores = scores + bias + mask_ref[step]
        expo = jnp.exp(scores - jnp.max(scores, axis=0, keepdims=True))
        probs = (expo * (1.0 / jnp.sum(expo, axis=0, keepdims=True))).astype(bf16)
        probs_ref[step, 0] = probs
        attended_ref[step, span, :] = dot_nn(value_ref[step, span, :], probs).astype(bf16)

    @pl.when(head == HEADS - 1)
    def _():
        place = iota((experts, TOK_MB), 0)
        each = len(block_refs) // MICRO
        for step in range(MICRO):
            hidden = x_ref[spans[step], :].astype(f32) + dot_tn(attended_ref[step], out_w[0])
            hidden_ref[step] = hidden
            scale = lax.rsqrt(jnp.mean(hidden * hidden, axis=-1, keepdims=True) + epsilon)
            rows = (hidden * scale * narrow_ref[experts + 1 : experts + 2, :].astype(f32)).astype(bf16)
            router = dot_nt(narrow_ref[:experts, :], rows)
            chosen = [
                jnp.sum(jnp.where(ids_ref[k : k + 1, spans[step]] == place, router, 0.0), axis=0, keepdims=True)
                for k in range(TOP)
            ]
            gates_ref[step, 0:1, :] = 1.0 / (1.0 + jnp.exp(chosen[1] - chosen[0]))
            gates_ref[step, 1:2, :] = 1.0 / (1.0 + jnp.exp(chosen[0] - chosen[1]))
            blocks = block_refs[step * each : (step + 1) * each]
            half = blocks[0].shape[0] // (4 // each)
            for first in range(0, 4 * half, half):
                hots = [slot_hot(slots_ref[step, k : k + 1, :], first, half) for k in range(TOP)]
                value = dot_nn(jnp.where(hots[0] | hots[1], 1.0, 0.0).astype(bf16), rows).astype(bf16)
                low = first // 2
                if each == 1:
                    blocks[0][first : first + half, :] = value
                else:
                    blocks[0][low : low + half // 2, :] = value[: half // 2]
                    blocks[1][low : low + half // 2, :] = value[half // 2 :]


def matrix_specs():
    return [
        pl.BlockSpec((1, D, D), functools.partial(lambda i, h: (i, 0, 0), i), pipeline_mode=pl.Buffered(1))
        for i in range(4)
    ]


def attend(starts, tokens, matrices, narrow, constants, ids, slots, direct, experts, capacity):
    size = experts * capacity // (1 + direct)
    out_shapes = (
        [((MICRO, D, TOK_MB), bf16)] * 3
        + [((MICRO, HEADS, SEQ_LEN, SEQ_LEN), bf16), ((MICRO, D, TOK_MB), bf16), ((MICRO, TOK_MB, D), f32)]
        + [((MICRO, TOP, TOK_MB), f32), ((MICRO, TOK_MB, D), bf16)]
        + [((size, D), bf16)] * (MICRO * (1 + direct))
    )

    def whole(shape):
        return resident(shape, lambda h: (0,) * len(shape))

    out_specs = [
        pl.BlockSpec((MICRO, 1, SEQ_LEN, SEQ_LEN), lambda h: (0, h, 0, 0)) if len(s) == 4 else whole(s)
        for s, _ in out_shapes
    ]
    return pl.pallas_call(
        functools.partial(attend_kernel, experts=experts),
        grid=(HEADS,),
        in_specs=[pl.BlockSpec(memory_space=pltpu.SMEM), whole(tokens.shape)]
        + matrix_specs()
        + [whole(a.shape) for a in (narrow, *constants, ids, slots)],
        out_specs=out_specs,
        out_shape=[jax.ShapeDtypeStruct(*s) for s in out_shapes],
        scratch_shapes=[pltpu.VMEM((MICRO, SEQ_LEN, SEQ_LEN), f32), pltpu.VMEM((16, 1024), f32)],
        compiler_params=pltpu.CompilerParams(vmem_limit_bytes=58 * MIB),
        cost_estimate=lasting(42),
        name="attend",
    )(starts, tokens, *[matrices] * 4, narrow, *constants, ids, slots)


def collect(target, direct, passed, size):
    if passed is None:
        for index, ref in enumerate(direct):
            target[index * ref.shape[0] : (index + 1) * ref.shape[0], :] = ref[...]
        return
    for index, ref in enumerate(direct):
        low = 2 * index * size
        target[low : low + size, :] = ref[...]
        target[low + size : low + 2 * size, :] = passed[index * size : (index + 1) * size, :]


def received_specs(received, blocks, size):
    first = lambda *_: (0, 0)
    return [resident((size, D), first)] * blocks + [resident(r.shape, first) for r in received[blocks:]]


def expert_kernel(place_ref, *refs, blocks, passes, micro):
    accumulate = micro > 0
    rows_refs, cot_refs, refs = refs[:blocks], refs[blocks : 2 * blocks + passes], refs[2 * blocks + passes :]
    other_ref, router_ref, in_ref, out_ref = refs[:4]
    refs = refs[4:]
    if accumulate:
        prior, refs = refs[:5], refs[5:]
    grads, refs = refs[:5], refs[5:]
    result_refs, back_refs = refs[:blocks], refs[blocks : 2 * blocks]
    rows, picks, rows_t, gate_column, result, back, active, inner_grad = refs[2 * blocks :]
    step, me = pl.program_id(0), place_ref[0]
    total, tile = rows.shape[0], ROW_TILE
    senders, capacity = other_ref.shape
    experts = grads[4].shape[0]
    width = capacity if passes else total
    place = iota((experts, width), 0)

    @pl.when(step == 0)
    def _():
        collect(rows, rows_refs, None, width)
        collect(picks, cot_refs[:blocks], cot_refs[blocks] if passes else None, width)
        for sender in range(senders):
            here = slice(sender * width, (sender + 1) * width)
            logits = dot_nt(router_ref[:experts, :], rows[here, :])
            other = other_ref[sender : sender + 1, :].astype(jnp.int32)
            own_logit = jnp.sum(jnp.where(place == me, logits, 0.0), axis=0, keepdims=True)
            other_logit = jnp.sum(jnp.where(place == other, logits, 0.0), axis=0, keepdims=True)
            column = row_to_column(1.0 / (1.0 + jnp.exp(other_logit - own_logit)))
            gate_column[here, :] = column
            picks[here, :] = (picks[here, :].astype(f32) * column).astype(bf16)
        for low in range(0, total, tile):
            rows_t[:, low : low + tile] = rows[low : low + tile, :].astype(f32).T.astype(bf16)
        result[...] = jnp.zeros_like(result)
        back[...] = jnp.zeros_like(back)

    def one_tile(index):
        here = slice(index * tile, (index + 1) * tile)
        inner = dot_nn(rows[here, :], in_ref[0])
        square = inner * inner
        bend = jnp.tanh(inner * (0.7978845608028654 + 0.035677408136300125 * square))
        half = 0.5 * inner
        low = (half + half * bend).astype(bf16)
        active[here, :] = low
        result[here, :] += dot_nn(low, out_ref[0])
        slope = 0.5 + 0.5 * bend + half * (1.0 - bend * bend) * (0.7978845608028654 + 0.1070322244089004 * square)
        grad = (dot_nt(picks[here, :], out_ref[0]) * slope).astype(bf16)
        inner_grad[here, :] = grad
        back[here, :] += dot_nt(grad, in_ref[0])

    for index in range(total // tile):
        one_tile(index)

    def store(index, where, value):
        if accumulate:
            value = value + prior[index][where].astype(f32)
        grads[index][where] = value.astype(bf16)

    quarter = D // 4
    for index in range(4):
        first = pl.multiple_of((index ^ place_ref[1]) * quarter, quarter)
        store(index // 2, index % 2, dot_nn(rows_t[pl.ds(first, quarter), :], inner_grad[...]))
    outer = dot_tn(active[...], picks[...])

    @pl.when(step >= 2)
    def _():
        store(2, 0, outer)

    @pl.when(step < 2)
    def _():
        store(3, 0, outer)

    @pl.when(step == pl.num_programs(0) - 1)
    def _():
        router_sum = prior[4][...] if accumulate else jnp.zeros((experts, D), f32)
        for sender in range(senders):
            here = slice(sender * width, (sender + 1) * width)
            low = result[here, :].astype(bf16)
            score = jnp.sum(low.astype(f32) * picks[here, :].astype(f32), axis=-1, keepdims=True)
            choice = column_to_row((1.0 - gate_column[here, :]) * score)
            other = other_ref[sender : sender + 1, :].astype(jnp.int32)
            logit_grad = jnp.where(place == me, choice, 0.0) - jnp.where(place == other, choice, 0.0)
            logit_grad = logit_grad.astype(bf16)
            router_sum = router_sum + dot_nn(logit_grad, rows[here, :])
            total_back = back[here, :] + dot_tn(logit_grad, router_ref[:experts, :])
            index, first = (sender // 2, sender % 2 * width) if passes else (0, 0)
            back_refs[index][first : first + width, :] = total_back.astype(bf16)
            result_refs[index][first : first + width, :] = low
        grads[4][...] = router_sum


def run_expert(place, rows_blocks, cot_blocks, other, narrow, expert_in, expert_out, prior, micro, blocks, experts):
    passes = len(cot_blocks) - blocks
    size = rows_blocks[0].shape[0]
    total = blocks * size
    fixed = lambda i, place: (0, 0)
    chunk, quarter = FF // 4, D // 4
    at = lambda i, place: i ^ 2 ^ place[2]
    weights = [
        pl.BlockSpec((1, D, chunk), lambda i, place: (0, 0, at(i, place))),
        pl.BlockSpec((1, chunk, D), lambda i, place: (0, at(i, place), 0)),
    ]
    grad_specs = [
        pl.BlockSpec((2, quarter, chunk), lambda i, place: (0, 0, at(i, place))),
        pl.BlockSpec((2, quarter, chunk), lambda i, place: (0, 0, at(i, place))),
        pl.BlockSpec((1, chunk, D), lambda i, place: (jnp.maximum(i - 2, 0), 0, 0)),
        pl.BlockSpec((1, chunk, D), lambda i, place: (jnp.minimum(i, 1), 0, 0)),
        resident((experts, D), fixed),
    ]
    grad_shapes = [((2, quarter, FF), bf16)] * 2 + [((2, chunk, D), bf16)] * 2 + [((experts, D), f32)]
    taken = received_specs(rows_blocks, blocks, size)
    taken += received_specs(cot_blocks, blocks, size // (1 + passes))
    out = pl.pallas_call(
        functools.partial(expert_kernel, blocks=blocks, passes=passes, micro=micro),
        grid_spec=pltpu.PrefetchScalarGridSpec(
            num_scalar_prefetch=1,
            grid=(4,),
            in_specs=taken
            + [resident(other.shape, fixed), resident(narrow.shape, fixed)]
            + weights
            + (grad_specs if prior else []),
            out_specs=grad_specs + [resident((size, D), fixed)] * (2 * blocks),
            scratch_shapes=[
                pltpu.VMEM((total, D), bf16),
                pltpu.VMEM((total, D), bf16),
                pltpu.VMEM((D, total), bf16),
                pltpu.VMEM((total, 1), f32),
                pltpu.VMEM((total, D), f32),
                pltpu.VMEM((total, D), f32),
                pltpu.VMEM((total, chunk), bf16),
                pltpu.VMEM((total, chunk), bf16),
            ],
        ),
        out_shape=[jax.ShapeDtypeStruct(*s) for s in grad_shapes]
        + [jax.ShapeDtypeStruct((size, D), bf16)] * (2 * blocks),
        compiler_params=pltpu.CompilerParams(vmem_limit_bytes=62 * MIB),
        cost_estimate=lasting(62),
        name="expert",
    )(place, *rows_blocks, *cot_blocks, other, narrow, expert_in, expert_out, *(prior or ()))
    return out[:5], out[5:]


def trade(value, groups, mask):
    return lax.ppermute(value, "group", swap(groups, mask))


def add_low(left, right):
    return (left.astype(f32) + right.astype(f32)).astype(bf16)


def second_half(half, groups, mask):
    return add_low(half[0], trade(half[1], groups, mask))


def spread_kernel(place_ref, own_ref, beside_ref, far_ref, out_ref, *, code):
    index = pl.program_id(0) ^ place_ref[code]

    @pl.when(index == 0)
    def _():
        out_ref[...] = own_ref[...].astype(f32)

    @pl.when(index == 1)
    def _():
        out_ref[...] = beside_ref[...].astype(f32)

    @pl.when(index > 1)
    def _():
        out_ref[...] = far_ref[...].astype(f32)


def spread_pieces(place, pieces, code):
    shape = pieces[0].shape[1:]
    block = (1, *shape)
    return pl.pallas_call(
        functools.partial(spread_kernel, code=code),
        grid_spec=pltpu.PrefetchScalarGridSpec(
            num_scalar_prefetch=1,
            grid=(4,),
            in_specs=[pl.BlockSpec(block, lambda i, place: (0, 0, 0))] * 2
            + [pl.BlockSpec(block, lambda i, place: ((i ^ place[code]) & 1, 0, 0))],
            out_specs=pl.BlockSpec(block, lambda i, place: (i, 0, 0)),
        ),
        out_shape=jax.ShapeDtypeStruct((4, *shape), f32),
        compiler_params=pltpu.CompilerParams(vmem_limit_bytes=32 * MIB),
        cost_estimate=lasting(6),
        name="spread",
    )(place, *pieces)


def back_kernel(*refs, blocks, passes, experts, devices, final):
    me_ref, refs = refs[0], refs[1:]
    take = blocks + passes
    back_refs, refs = refs[:take], refs[take:]
    (x_ref, cot_ref, query_w, key_w, value_w, out_w, narrow_ref, hot_ref, bucket_ref, heads_ref, slots_ref) = refs[:11]
    (query_ref, key_ref, value_ref, probs_ref, attended_ref, hidden_ref, normed_ref) = refs[11:18]
    refs = refs[18:]
    if final:
        prior, router_grad, refs = refs[: 1 + passes], refs[1 + passes], refs[2 + passes :]
    token_ref, dense_refs, refs = refs[0], refs[1 : 2 + passes], refs[2 + passes :]
    gathered, hidden_grad, out_grad, query_grad, key_grad, value_grad, whole, lines, diagonals = refs
    head = pl.program_id(0)
    total = gathered.shape[0]

    def dense(first, value):
        columns = slice(first, first + value.shape[1])
        if not passes:
            if final:
                value = value + prior[0][:, columns].astype(f32)
            dense_refs[0][:, columns] = value.astype(bf16)
            return
        whole[:, : value.shape[1]] = value
        rows = D // devices
        for k in range(devices):
            start = pl.multiple_of((me_ref[0] ^ k) * rows, 32)
            piece = whole[pl.ds(start, rows), : value.shape[1]]
            here = slice(k // 2 * rows, (k // 2 + 1) * rows)
            if final:
                piece = piece + prior[k % 2][here, columns].astype(f32)
            dense_refs[k % 2][here, columns] = piece.astype(bf16)

    @pl.when(head == 0)
    def _():
        lines[...] = jnp.zeros_like(lines)
        diagonals[...] = jnp.zeros_like(diagonals)
        cot = cot_ref[...].astype(f32)
        collect(gathered, back_refs[:blocks], back_refs[blocks] if passes else None, back_refs[0].shape[0])
        columns = [row_to_column(slots_ref[k : k + 1, :].astype(f32)).astype(jnp.int32) for k in range(TOP)]
        rows_grad = jnp.zeros((TOK_MB, D), f32)
        for low in range(0, total, 512):
            place = iota((TOK_MB, 512), 1) + low
            pick = jnp.where((place == columns[0]) | (place == columns[1]), 1.0, 0.0).astype(bf16)
            rows_grad = rows_grad + dot_nn(pick, gathered[low : low + 512, :])
        hidden = hidden_ref[...]
        scale = lax.rsqrt(jnp.mean(hidden * hidden, axis=-1, keepdims=True) + epsilon)
        normal = hidden * scale
        lines[experts + 1 : experts + 2, :] = jnp.sum(rows_grad * normal, axis=0, keepdims=True)
        scaled = rows_grad * narrow_ref[experts + 1 : experts + 2, :].astype(f32)
        total_grad = cot + scale * (scaled - normal * jnp.mean(scaled * normal, axis=-1, keepdims=True))
        hidden_grad[...] = total_grad
        branch = total_grad.astype(bf16)
        dense(3 * D, dot_nn(attended_ref[...], branch))
        out_grad[...] = dot_nt(out_w[0], branch).astype(bf16)

    span = pl.ds(pl.multiple_of(head * HEAD_DIM, HEAD_DIM), HEAD_DIM)
    low = probs_ref[0]
    grad_here = out_grad[span, :]
    probs = low.astype(f32)
    value_grad[span, :] = dot_nt(grad_here, low).astype(bf16)
    prob_grad = dot_tn(value_ref[span, :], grad_here)
    center = jnp.sum(probs * prob_grad, axis=0, keepdims=True)
    score_grad = (probs * (prob_grad - center)).astype(bf16)
    query_grad[span, :] = (dot_nn(key_ref[span, :], score_grad) * HEAD_DIM**-0.5).astype(bf16)
    key_grad[span, :] = dot_nt(query_ref[span, :], score_grad).astype(bf16)
    wide = score_grad.astype(f32)
    chunks = []
    for place in range(-3, 4):
        parts = [
            wide[a * 128 : a * 128 + 128, (a + place) * 128 : (a + place) * 128 + 128]
            for a in range(4)
            if 0 <= a + place < 4
        ]
        chunks.append(sum(parts[1:], parts[0]))
    folded = jnp.concatenate([*chunks, jnp.zeros((128, 128), f32)], axis=1)
    for half in (64, 32, 16, 8):
        folded = folded[:half] + pltpu.roll(folded[half:], 1024 - half, 1)
    low_row = iota((8, 1024), 0)
    for bit in (4, 2, 1):
        folded = jnp.where((low_row & bit) != 0, pltpu.roll(folded, 1024 - bit, 1), folded)
    diagonals[pl.ds(head, 1), :] = jnp.sum(folded, axis=0, keepdims=True)

    @pl.when(head == HEADS - 1)
    def _():
        normed_t = normed_ref[...].astype(f32).T.astype(bf16)
        grads = (query_grad[...], key_grad[...], value_grad[...])
        in_grad = jnp.zeros((D, TOK_MB), f32)
        for i, (grad, weight) in enumerate(zip(grads, (query_w, key_w, value_w))):
            dense(i * D, dot_nt(normed_t, grad))
            in_grad = in_grad + dot_nn(weight[0], grad)
        in_grad = in_grad.T
        x = x_ref[...].astype(f32)
        scale = lax.rsqrt(jnp.mean(x * x, axis=-1, keepdims=True) + epsilon)
        normal = x * scale
        lines[experts : experts + 1, :] = jnp.sum(in_grad * normal, axis=0, keepdims=True)
        scaled = in_grad * narrow_ref[experts : experts + 1, :].astype(f32)
        grad = hidden_grad[...] + scale * (scaled - normal * jnp.mean(scaled * normal, axis=-1, keepdims=True))
        token_ref[...] = grad.astype(bf16)
        if final:
            lines[:experts, :] = router_grad[...]
        by_bucket = sum_dot(diagonals[...], hot_ref[...], dot_nt)
        by_place = sum_dot(by_bucket, bucket_ref[...], dot_nt)
        lines[experts + 2 : experts + 3, :] = jnp.sum(by_place * heads_ref[...].astype(f32), axis=0, keepdims=True)
        dense(4 * D, lines[...].T)


def sum_dot(values, hot, dot):
    high = values.astype(bf16)
    return dot(high, hot) + dot((values - high.astype(f32)).astype(bf16), hot)


def backward(me, back_blocks, tokens, cotangent, matrices, narrow, constants, slots, saved, prior, step, blocks, experts, devices, slot_count):
    passes = len(back_blocks) - blocks
    size = slot_count // blocks // (1 + passes)
    fixed = lambda h: (0, 0)
    block = lambda h: (step, 0)
    head_block = pl.BlockSpec((None, 1, SEQ_LEN, SEQ_LEN), lambda h: (step, h, 0, 0))
    wide = 4 * D + 128
    dense_shapes = [(D // (1 + passes), wide)] * (1 + passes)
    dense_specs = [resident(s, fixed) for s in dense_shapes]
    return pl.pallas_call(
        functools.partial(
            back_kernel, blocks=blocks, passes=passes, experts=experts, devices=devices, final=prior is not None
        ),
        grid=(HEADS,),
        in_specs=[pl.BlockSpec(memory_space=pltpu.SMEM)]
        + received_specs(back_blocks, blocks, size)
        + [resident((TOK_MB, D), block)] * 2
        + matrix_specs()
        + [resident(narrow.shape, fixed)]
        + [resident(c.shape, fixed) for c in constants]
        + [resident((TOP, TOK_MB), fixed)]
        + [head_block if s.ndim == 4 else resident((None, *s.shape[1:]), lambda h: (step, 0, 0)) for s in saved]
        + (dense_specs + [resident((experts, D), fixed)] if prior else []),
        out_specs=[resident((TOK_MB, D), fixed)] + dense_specs,
        out_shape=[jax.ShapeDtypeStruct((TOK_MB, D), bf16)] + [jax.ShapeDtypeStruct(s, bf16) for s in dense_shapes],
        scratch_shapes=[
            pltpu.VMEM((slot_count, D), bf16),
            pltpu.VMEM((TOK_MB, D), f32),
            pltpu.VMEM((D, TOK_MB), bf16),
            pltpu.VMEM((D, TOK_MB), bf16),
            pltpu.VMEM((D, TOK_MB), bf16),
            pltpu.VMEM((D, TOK_MB), bf16),
            pltpu.VMEM((D, D), f32),
            pltpu.VMEM((128, D), f32),
            pltpu.VMEM((16, 1024), f32),
        ],
        compiler_params=pltpu.CompilerParams(vmem_limit_bytes=58 * MIB),
        cost_estimate=lasting(34),
        name="backward",
    )(me, *back_blocks, tokens, cotangent, *[matrices] * 4, narrow, *constants, slots, *saved, *(prior or ()))


def combine_kernel(*refs, blocks, passes):
    result_refs = refs[: blocks + passes]
    hidden_ref, slots_ref, gates_ref, mixed_ref, gathered = refs[blocks + passes :]
    size = result_refs[0].shape[0]
    collect(gathered, result_refs[:blocks], result_refs[blocks] if passes else None, size)
    slots = [row_to_column(slots_ref[k : k + 1, :].astype(f32)).astype(jnp.int32) for k in range(TOP)]
    gates = [row_to_column(gates_ref[k : k + 1, :]) for k in range(TOP)]
    output = hidden_ref[...]
    for k in range(TOP):
        picked = jnp.zeros((TOK_MB, D), f32)
        for low in range(0, gathered.shape[0], 512):
            pick = jnp.where(iota((TOK_MB, 512), 1) + low == slots[k], 1.0, 0.0).astype(bf16)
            picked = picked + dot_nn(pick, gathered[low : low + 512, :])
        output = output + gates[k] * picked
    mixed_ref[...] = output.astype(bf16)


def combine(received, hidden, slots, gates, step, blocks, slot_count):
    passes = len(received) - blocks
    size = slot_count // blocks // (1 + passes)
    fixed = lambda i: (0, 0)
    return pl.pallas_call(
        functools.partial(combine_kernel, blocks=blocks, passes=passes),
        grid=(1,),
        in_specs=received_specs(received, blocks, size)
        + [resident((None, *a.shape[1:]), lambda i: (step, 0, 0)) for a in (hidden, slots, gates)],
        out_specs=resident((TOK_MB, D), fixed),
        out_shape=jax.ShapeDtypeStruct((TOK_MB, D), bf16),
        scratch_shapes=[pltpu.VMEM((slot_count, D), bf16)],
        compiler_params=pltpu.CompilerParams(vmem_limit_bytes=32 * MIB),
        cost_estimate=lasting(3),
        name="combine",
    )(*received, hidden, slots, gates)


def tie(values, *after):
    count = len(values)
    return list(lax.optimization_barrier((*values, *after)))[:count]


def send(blocks, devices):
    if len(blocks) == 1:
        whole = blocks[0]
        moved = whole.reshape(devices, -1, D)
        moved = lax.all_to_all(moved, "expert", split_axis=0, concat_axis=0, tiled=True)
        return [moved.reshape(whole.shape)]
    return [blocks[0]] + [
        lax.ppermute(blocks[j], "expert", swap(devices, 2 * j)) for j in range(1, len(blocks))
    ]


def pair_up(near, cross, devices):
    got = lax.ppermute(cross, "expert", swap(devices, 1))
    size = 2 * near.shape[0] // devices
    return [jnp.concatenate([a[low : low + size] for a in (near, got)]) for low in range(0, near.shape[0], size)]


def pass_on(blocks, devices):
    if len(blocks) == 1:
        return blocks
    half = blocks[0].shape[0] // 2
    second = jnp.concatenate([b[half:] for b in blocks], axis=0)
    return [*blocks, lax.ppermute(second, "expert", swap(devices, 1))]


def sum_cores(pieces, devices):
    near, cross = pieces
    return near.astype(f32) + lax.ppermute(cross, "expert", swap(devices, 1)).astype(f32)


def sum_chips(own, low, devices):
    chips = devices // 2
    rows = low.shape[0] // chips
    for j in range(1, chips):
        own = own + lax.ppermute(low[j * rows : (j + 1) * rows], "expert", swap(devices, 2 * j)).astype(f32)
    return own


def reduce_group(total, groups, *after):
    parts, masks = [total[:, : 2 * D], total[:, 2 * D :]], [1, 2]
    for turn in range(2):
        low = [part.astype(bf16) for part in parts]
        if turn:
            low = tie(low, *after)
        parts = [
            here.astype(f32) + lax.ppermute(here, "group", swap(groups, mask)).astype(f32)
            for here, mask in zip(low, masks)
        ]
        masks = masks[::-1]
    return parts


def shards(
    tokens, cotangent, norm_attn, w_query, w_key, w_value, w_out, rel_bias, norm_expert, w_router,
    expert_in, expert_out, expert_ids, span_starts,
):
    experts = w_router.shape[1]
    capacity = 3 * TOK_MB * TOP // (2 * experts)
    groups, devices = lax.axis_size("group"), lax.axis_size("expert")
    direct = devices <= DIRECT_MAX
    blocks = devices // 2 if direct else 1
    shard, share = w_query.shape[0], rel_bias.shape[0]
    me = lax.axis_index("expert").reshape(1).astype(jnp.int32)
    order = me if direct else jnp.zeros_like(me)
    ids = expert_ids.T
    group = lax.axis_index("group").reshape(1).astype(jnp.int32)
    place = jnp.concatenate([me, group % 2 * 2 + group // 2, group])

    padded = jnp.pad(rel_bias, (0, shard - share))
    narrow = jnp.concatenate([w_router.T, norm_attn[None], norm_expert[None], padded[None]], axis=0)
    slots, cots = route(order, ids, cotangent, blocks, experts, capacity)
    matrices, narrow, all_ids, cots[0] = gather_weights(
        (w_query, w_key, w_value, w_out), narrow, ids, cots[0], groups, devices
    )
    bucket, heads = bias_places(devices)
    constants = (bucket_hot().astype(bf16), bucket.astype(bf16), heads.astype(bf16))
    slot_count = experts * capacity
    cots[1] = send(tie(cots[1], *cots[0][1:]), devices)
    other = partners(me, all_ids, devices, capacity, direct)
    if not direct:
        other = other.reshape(MICRO, 1, slot_count)
    (narrow,) = tie([narrow], *cots[0][1:], other)
    *saved, = attend(span_starts, tokens, matrices, narrow, constants, ids, slots, direct, experts, capacity)
    saved, sent = saved[:8], saved[8:]
    sent = [sent[step * (1 + direct) : (step + 1) * (1 + direct)] for step in range(MICRO)]
    cots[1] = tie(cots[1], saved[0])
    if direct:
        sent = [pair_up(*tie(s, *cots[1][1:]), devices) for s in sent]
    sent[0] = send(tie(sent[0], *cots[1][1:]), devices)
    cots = [pass_on(tie(c, saved[0]), devices) for c in cots]
    sent[1] = send(tie(sent[1], *sent[0][1:]), devices)

    grads, first = run_expert(
        place, sent[0], cots[0], other[0], narrow, expert_in, expert_out, None, 0, blocks, experts
    )
    sent[1] = tie(sent[1], first[0])
    results, backs = [first[:blocks]], [send(tie(first[blocks:], *sent[1]), devices)]
    grads, last = run_expert(
        place, sent[1], cots[1], other[1], narrow, expert_in, expert_out, grads, 1, blocks, experts
    )
    results.append(last[:blocks])
    backs.append(last[blocks:])
    *flat, router_grad = tie(grads, *backs[0][1:])
    away = [trade(flat[1], groups, 1), trade(flat[3], groups, 2)]
    backs[0] = tie(backs[0], last[0])
    backs[1] = send(tie(backs[1], *backs[0][1:]), devices)
    backs[0] = pass_on(backs[0], devices)

    def run_back(step, prior):
        query, key, value, probs, attended, hidden, _, normed = saved
        return backward(
            order, backs[step], tokens, cotangent, matrices, narrow, constants, slots[step],
            (query, key, value, probs, attended, hidden, normed), prior, step, blocks, experts, devices, slot_count,
        )

    token_grads = [None, None]
    token_grads[0], *dense = run_back(0, None)
    backs[1] = pass_on(tie(backs[1], token_grads[0]), devices)
    away = tie(away, *backs[1])
    halves = [add_low(flat[0], away[0]), add_low(flat[2], away[1])]
    owns = [second_half(halves[0], groups, 2), second_half(halves[1], groups, 1)]
    if direct:
        results[0] = send(tie(results[0], *backs[1]), devices)
    else:
        results = [send(r, devices) for r in results]
    backs[1] = tie(backs[1], *halves)
    token_grads[1], *dense = run_back(1, (*dense, router_grad))
    owns = tie(owns, token_grads[1], *results[0])
    if direct:
        results[0] = pass_on(tie(results[0], token_grads[1]), devices)
    if direct:
        dense = tie(dense, *results[0][1:-1], *owns)
        total = sum_cores(dense, devices)
        low = total.astype(bf16)
        owns = tie(owns, low)
    besides = [trade(owns[0], groups, 2), trade(owns[1], groups, 1)]
    fars = [jnp.stack(pair) for pair in zip(owns, besides)]
    if direct:
        total = sum_chips(total[:shard], low, devices)
        results[1] = send(tie(results[1], total), devices)
        (total,) = tie([total], results[1][1])
        results[1] = pass_on(results[1], devices)
    else:
        total = lax.psum_scatter(dense[0], "expert", scatter_dimension=0, tiled=True).astype(f32)
    fars = [trade(fars[0], groups, 1), trade(fars[1], groups, 2)]
    inward, outward = [(own[None], beside[None], far) for own, beside, far in zip(owns, besides, fars)]
    mixed = [
        combine(results[step], saved[5], slots, saved[6], step, blocks, slot_count)
        for step in range(MICRO)
    ]
    (total,) = tie([total], mixed[0])
    grad_in = spread_pieces(place, inward, 1).reshape(expert_in.shape)
    grad_out = spread_pieces(place, outward, 2).reshape(expert_out.shape)
    total = reduce_group(total, groups, grad_in, grad_out)
    first, second = total
    thin = second[:, 2 * D :]
    return (
        jnp.concatenate(mixed, axis=0),
        jnp.concatenate(token_grads, axis=0),
        thin[:, experts],
        first[:, :D],
        first[:, D:],
        second[:, :D],
        second[:, D : 2 * D],
        thin[:share, experts + 2],
        thin[:, experts + 1],
        thin[:, :experts],
        grad_in,
        grad_out,
    )


def solution(mesh):
    rows, split = P(("group", "expert"), None), P("expert", None)
    stacked = P("expert", None, None)
    return jax.shard_map(
        shards,
        mesh=mesh,
        in_specs=(
            rows, rows, P("expert"), split, split, split, split, P("expert"), P("expert"), split,
            stacked, stacked, rows, P(("group", "expert")),
        ),
        out_specs=(
            rows, rows, P("expert"), split, split, split, split, P("expert"), P("expert"), split, stacked, stacked,
        ),
        check_vma=False,
    )
```
